256 devices in a mesh: chan: 32 (over y_lo, z, core), seq: 8 (over y_hi, x).
Axes of the slice: x: 4, y: 4 (y_hi: 2, y_lo: 2; y = y_hi * 2 + y_lo), z: 8, core: 2. Of those that a mesh axis runs over, the one named last changes fastest.
Arguments:
- query_input: bfloat16 [8192, 8192], P('seq', 'chan'), may hold values from -6 to 6
- key_input: bfloat16 [8192, 8192], P('seq', 'chan'), may hold values from -6 to 6
- value_input: bfloat16 [8192, 8192], P('seq', 'chan'), may hold values from -6 to 6
- filter_spectrum: bfloat16 [1024, 16, 2, 8192], P('seq', None, None, 'chan'), may hold values from -6 to 6
- out_weight: bfloat16 [8192, 8192], P('chan'), may hold values from -0.125 to 0.125
Outputs:
- mixed: bfloat16 [8192, 8192], P('chan', 'seq')
The draws below stay inside these ranges and needn't reach their ends.
All inputs are finite; a program needn't handle non-finite values.
Results may differ from the reference program's by a relative error of at most 0.03.
Values may be sent and summed in bfloat16 or wider, within the bound.
A program may use at most 128 MiB of HBM per device.

```python
import math
import jax
import jax.numpy as jnp
from jax import lax

P_SIZE = 1024
C_DEV = 256
D_OUT = 8192
C = 8192
SEQ_LEN = 8192
FFT_LEN = 16384
Q = 16
N_CHAN = 32


def with_spikes(result, rng, source, target, shards_of, factor):
    owner, partner = [(jnp.arange(result.shape[dim]) // (result.shape[dim] // shards_of)).reshape([-1 if axis == dim else 1 for axis in range(result.ndim)]) for dim in (source, target)]
    chosen = jax.random.permutation(rng, shards_of)[partner]
    strong = (owner == chosen) | (owner == (partner + shards_of // 2) % shards_of)
    return jnp.where(strong, factor * result, result)


def steps_of(rng, dims, shards, low, high):
    gain, own = 1.0, jax.random.fold_in(rng, 6)
    for axis_at, shards_of in shards:
        heights = jnp.exp(jax.random.uniform(jax.random.fold_in(own, axis_at), (shards_of,), jnp.float32, low / len(shards), high / len(shards)))
        gain = gain * jnp.repeat(heights, dims[axis_at] // shards_of).reshape([-1 if axis == axis_at else 1 for axis in range(len(dims))])
    return gain


def normal_values(key, shape, spread, most, split=(), held_as=jnp.bfloat16):
    values = spread * jax.random.normal(key, shape, jnp.float32)
    if split:
        values = values * steps_of(key, shape, split, -0.22, 0.18)
    return jnp.clip(values, -most, most).astype(held_as)


def noise_with(own_key, extent, scale, reach, shards, heavy, dtype=jnp.bfloat16):
    drawn = scale * jax.random.normal(own_key, extent, jnp.float32)
    if shards:
        drawn = drawn * steps_of(own_key, extent, shards, -0.22, 0.18)
    return jnp.clip(with_spikes(drawn, jax.random.fold_in(own_key, 3), *heavy), -reach, reach).astype(dtype)


def setup_inputs(seed: int = 0) -> dict:
    streams_of = jax.random.split(jax.random.key(seed), 6)
    return {
        "query_input": normal_values(streams_of[0], (SEQ_LEN, C), 1.0, 6.0, ((0, 8), (1, 32))),
        "key_input": normal_values(streams_of[1], (SEQ_LEN, C), 1.0, 6.0, ((0, 8), (1, 32))),
        "value_input": normal_values(streams_of[2], (SEQ_LEN, C), 1.0, 6.0, ((0, 8), (1, 32))),
        "filter_spectrum": normal_values(streams_of[3], (P_SIZE, Q, 2, C), 1.0, 6.0, ((0, 8), (3, 32))),
        "out_weight": noise_with(streams_of[4], (C, D_OUT), C ** -0.5, 0.125, ((0, 32),), (0, 1, 32, 2.75)),
    }


def angle_table(rows, cols, modulus, row_first, col_first):
    row_ids = row_first + lax.iota(jnp.int32, rows)
    col_ids = col_first + lax.iota(jnp.int32, cols)
    product = (row_ids[:, None] * col_ids[None, :]) % modulus
    return (2.0 * math.pi / modulus) * product.astype(jnp.float32)


def block_tables(order):
    angles = angle_table(order, order // 2, order, 0, 0)
    return jnp.cos(angles).astype(jnp.bfloat16), jnp.sin(angles).astype(jnp.bfloat16)


def first_section(values, total_len):
    half, count, width = values.shape
    order = 2 * half
    cosine, sine = block_tables(order)
    flat = values.reshape(half, count * width)
    real_part = jnp.dot(cosine, flat, preferred_element_type=jnp.float32).reshape(order, count, width)
    imag_part = -jnp.dot(sine, flat, preferred_element_type=jnp.float32).reshape(order, count, width)
    angles = angle_table(order, count, total_len, 0, 0)[:, :, None]
    tw_cos = jnp.cos(angles)
    tw_sin = jnp.sin(angles)
    twist_real = real_part * tw_cos + imag_part * tw_sin
    twist_imag = imag_part * tw_cos - real_part * tw_sin
    return jnp.stack([twist_real, twist_imag]).astype(jnp.bfloat16)


def mix(field, table):
    return jnp.einsum("knc,nm->kmc", field.astype(jnp.float32), table.astype(jnp.float32))


def middle_section(spectrum, filt, total_len):
    rows = spectrum.shape[1]
    length = spectrum.shape[2]
    short = angle_table(length, length, length, 0, 0)
    short_cos = jnp.cos(short).astype(jnp.bfloat16)
    short_sin = jnp.sin(short).astype(jnp.bfloat16)
    real_in = spectrum[0]
    imag_in = spectrum[1]
    freq_real = mix(real_in, short_cos) + mix(imag_in, short_sin)
    freq_imag = mix(imag_in, short_cos) - mix(real_in, short_sin)
    filt_real = filt[:, :, 0].astype(jnp.float32)
    filt_imag = filt[:, :, 1].astype(jnp.float32)
    prod_real = (freq_real * filt_real - freq_imag * filt_imag).astype(jnp.bfloat16)
    prod_imag = (freq_real * filt_imag + freq_imag * filt_real).astype(jnp.bfloat16)
    back_real = mix(prod_real, short_cos) - mix(prod_imag, short_sin)
    back_imag = mix(prod_imag, short_cos) + mix(prod_real, short_sin)
    angles = angle_table(rows, length, total_len, 0, 0)[:, :, None]
    tw_cos = jnp.cos(angles)
    tw_sin = jnp.sin(angles)
    out_real = back_real * tw_cos - back_imag * tw_sin
    out_imag = back_imag * tw_cos + back_real * tw_sin
    return jnp.stack([out_real, out_imag]).astype(jnp.bfloat16)


def last_section(spectrum, total_len):
    order = spectrum.shape[1]
    count = spectrum.shape[2]
    width = spectrum.shape[3]
    cosine, sine = block_tables(order)
    flat_real = spectrum[0].reshape(order, count * width)
    flat_imag = spectrum[1].reshape(order, count * width)
    signal = jnp.dot(cosine.T, flat_real, preferred_element_type=jnp.float32)
    signal = signal - jnp.dot(sine.T, flat_imag, preferred_element_type=jnp.float32)
    signal = signal * (1.0 / total_len)
    return signal.astype(jnp.bfloat16).reshape(order // 2, count, width)


def reference(query_input, key_input, value_input, filter_spectrum, out_weight):
    def regroup(array):
        return array.reshape(SEQ_LEN, N_CHAN, C_DEV).transpose(1, 0, 2)

    filters = filter_spectrum.reshape(P_SIZE, Q, 2, N_CHAN, C_DEV).transpose(3, 0, 1, 2, 4)
    weights = out_weight.reshape(N_CHAN, C_DEV, D_OUT)

    def step(total, inputs):
        query_part, key_part, value_part, filt, weight = inputs
        product = (key_part.astype(jnp.float32) * value_part.astype(jnp.float32)).astype(jnp.bfloat16)
        first = first_section(product.reshape(P_SIZE // 2, Q, C_DEV), FFT_LEN)
        middle = middle_section(first, filt, FFT_LEN)
        signal = last_section(middle, FFT_LEN).reshape(SEQ_LEN, C_DEV)
        gated = (query_part.astype(jnp.float32) * signal.astype(jnp.float32)).astype(jnp.bfloat16)
        partial_value = jnp.dot(gated, weight, preferred_element_type=jnp.float32).astype(jnp.bfloat16)
        partial_value = lax.optimization_barrier(partial_value).astype(jnp.float32)
        return total + partial_value, None

    start = jnp.zeros((SEQ_LEN, D_OUT), jnp.float32)
    total, _ = lax.scan(step, start, (regroup(query_input), regroup(key_input), regroup(value_input), filters, weights))
    return total.T.astype(jnp.bfloat16)
```

```python
import functools
import math

import jax
import jax.numpy as jnp
import ml_dtypes
import numpy as np
from jax import lax
from jax.experimental import pallas as pl
from jax.experimental.pallas import tpu as pltpu
from jax.sharding import PartitionSpec as P

BF = jnp.bfloat16
F32 = jnp.float32
ORDER = 1024
SHORT = 16
TOTAL = ORDER * SHORT
SEQ = 8
SUB = 32
LANES = SHORT * SUB
MESH = pl.DeviceIdType.MESH
QUARTER = 256
ORDER_OF_QUARTERS = (0, 2, 1, 3)


def make_tables():
    step = np.arange(ORDER)
    angle = 2.0 * math.pi / ORDER * (np.outer(step, step) % ORDER)
    long_cos = np.cos(angle)
    long_nsin = -np.sin(angle)
    short = np.arange(SHORT)
    angle = 2.0 * math.pi / SHORT * (np.outer(short, short) % SHORT)
    eye = np.eye(SUB)
    short_cos = np.kron(np.cos(angle), eye)
    short_sin = np.kron(np.sin(angle), eye)
    forth = np.block([[short_cos, -short_sin], [short_sin, short_cos]])
    back = np.block([[short_cos, short_sin], [-short_sin, short_cos]])
    angle = 2.0 * math.pi / TOTAL * np.outer(step, short)
    twist_cos = np.repeat(np.cos(angle), SUB, axis=1)
    twist_sin = np.repeat(np.sin(angle), SUB, axis=1)
    rows = np.zeros((512, 512))
    first, second = np.meshgrid(np.arange(32), np.arange(16), indexing="ij")
    rows[(second * 32 + first).ravel(), (first * 16 + second).ravel()] = 1.0
    lanes = np.zeros((512, 512))
    outer, inner, chan = np.meshgrid(np.arange(4), np.arange(4), np.arange(32), indexing="ij")
    lanes[
        (outer * 128 + inner * 32 + chan).ravel(), (inner * 128 + outer * 32 + chan).ravel()
    ] = 1.0

    def half(array):
        return array.astype(np.float32).astype(ml_dtypes.bfloat16)

    return (
        half(np.stack([rows, rows.T, lanes])),
        half(np.stack([long_cos, long_nsin])),
        np.stack([twist_cos, twist_sin]).astype(np.float32),
        half(np.stack([forth, back])),
    )


def dot(left, right):
    return jnp.dot(left, right, preferred_element_type=F32)


def arrive(ref, sem):
    pltpu.make_async_copy(ref, ref, sem).wait()


def kernel(
    query,
    key,
    value,
    filt,
    weight,
    moves,
    long_table,
    twist,
    short_table,
    out,
    query_v,
    key_v,
    value_v,
    filt_v,
    moves_v,
    long_v,
    twist_v,
    short_v,
    sorted_v,
    prod_send,
    prod_recv,
    filt_send,
    filt_recv,
    field,
    total,
    conv_send,
    conv_recv,
    gated,
    weights,
    ring_send,
    ring_recv,
    local_sem,
    prod_ss,
    prod_rs,
    filt_ss,
    filt_rs,
    conv_ss,
    conv_rs,
    weight_ss,
    weight_rs,
    gate_ss,
    gate_rs,
    ring_ss,
    ring_rs,
):
    chan = lax.axis_index("chan")
    me = lax.axis_index("seq")
    y_lo, z, core = chan // 16, (chan // 2) % 8, chan % 2
    y_hi, x = me // 4, me % 4

    def chan_of(low, depth, which):
        return (low * 8 + depth) * 2 + which

    sibling = {"chan": chan_of(y_lo, z, 1 - core), "seq": me}
    across = {"chan": chan_of(1 - y_lo, z, core), "seq": me}
    far = (1 - y_hi) * 4 + x
    z_up = (z + 1) % 8
    z_down = (z + 7) % 8
    up = {"chan": chan_of(y_lo, z_up, core), "seq": me}
    down = {"chan": chan_of(y_lo, z_down, core), "seq": me}

    local = [
        (key, key_v),
        (value, value_v),
        (moves, moves_v),
        (filt, filt_v),
        (long_table, long_v),
        (twist, twist_v),
        (short_table, short_v),
        (query, query_v),
    ]
    for at, (source, target) in enumerate(local):
        pltpu.make_async_copy(source, target, local_sem.at[at]).start()

    def local_done(at):
        pltpu.make_async_copy(local[at][0], local[at][1], local_sem.at[at]).wait()

    barrier = pltpu.get_barrier_semaphore()

    def greet(step, carry):
        peer = (me + step) % SEQ
        pl.semaphore_signal(barrier, 1, device_id={"chan": chan, "seq": peer}, device_id_type=MESH)
        return carry

    lax.fori_loop(1, SEQ, greet, 0)
    for peer in (
        sibling,
        up,
        down,
        across,
        {"chan": chan_of(1 - y_lo, z, 1 - core), "seq": me},
        {"chan": chan_of(1 - y_lo, z, core), "seq": far},
        {"chan": chan_of(1 - y_lo, z, 1 - core), "seq": far},
    ):
        pl.semaphore_signal(barrier, 1, device_id=peer, device_id_type=MESH)

    local_done(0)
    local_done(1)
    local_done(2)
    for half in range(2):
        rows = pl.ds(half * 512, 512)
        product = (key_v[rows, :].astype(F32) * value_v[rows, :].astype(F32)).astype(BF)
        moved = dot(moves_v[0], product).astype(BF)
        sorted_v[:, pl.ds(half * 32, 32), :] = moved.reshape(SHORT, 32, 256)
    for tile in range(2):
        block = jnp.concatenate(
            [
                jnp.concatenate(
                    [sorted_v[4 * group + b, :, pl.ds(tile * 128, 128)] for b in range(4)], axis=1
                )
                for group in range(4)
            ],
            axis=0,
        )
        moved = dot(block, moves_v[2]).astype(BF)
        for owner in range(4):
            for group in range(4):
                prod_send[4 * tile + owner, :, pl.ds(group * 128, 128)] = moved[
                    group * 64 : (group + 1) * 64, owner * 128 : (owner + 1) * 128
                ]
    pl.semaphore_wait(barrier, SEQ - 1 + 7)

    def spread(send, recv, ss, rs):
        def one(step, carry):
            peer = (me + step) % SEQ
            pltpu.make_async_remote_copy(
                send.at[peer],
                recv.at[me],
                ss.at[peer],
                rs.at[me],
                device_id={"chan": chan, "seq": peer},
                device_id_type=MESH,
            ).start()
            return carry

        lax.fori_loop(1, SEQ, one, 0)
        pltpu.make_async_copy(send.at[me], recv.at[me], rs.at[me]).start()

    def spread_done(send, ss):
        def one(step, carry):
            peer = (me + step) % SEQ
            arrive(send.at[peer], ss.at[peer])
            return carry

        lax.fori_loop(1, SEQ, one, 0)

    spread(prod_send, prod_recv, prod_ss, prod_rs)

    local_done(3)

    def sort_filter(group, carry):
        for tile in range(2):
            block = jnp.concatenate(
                [
                    jnp.concatenate(
                        [filt_v[part, 4 * group + b, :, pl.ds(tile * 128, 128)] for b in range(4)],
                        axis=1,
                    )
                    for part in range(2)
                ],
                axis=0,
            )
            moved = dot(block, moves_v[2]).astype(BF)
            lanes = pl.ds(pl.multiple_of(group * 128, 128), 128)
            for owner in range(4):
                for part in range(2):
                    filt_send[4 * tile + owner, part, :, lanes] = moved[
                        part * 128 : (part + 1) * 128, owner * 128 : (owner + 1) * 128
                    ]
        return carry

    lax.fori_loop(0, 4, sort_filter, 0)
    spread(filt_send, filt_recv, filt_ss, filt_rs)

    def weight_block(low, depth, which):
        at = pl.multiple_of(chan_of(low, depth, which) * 256, 256)
        return weight.at[:, pl.ds(at, 256)]

    def send_weight(depth, carry):
        pltpu.make_async_copy(
            weight_block(y_lo, depth, core), weights.at[depth, pl.ds(0, 256), :], weight_rs.at[depth]
        ).start()
        pltpu.make_async_remote_copy(
            weight_block(y_lo, depth, 1 - core),
            weights.at[depth, pl.ds(256, 256), :],
            weight_ss,
            weight_rs.at[depth],
            device_id=sibling,
            device_id_type=MESH,
        ).start()
        seq_to = ((y_hi + depth) % 2) * 4 + x
        for slot, which in ((2, core), (3, 1 - core)):
            pltpu.make_async_remote_copy(
                weight_block(1 - y_lo, depth, which),
                weights.at[depth, pl.ds(slot * 256, 256), :],
                weight_ss,
                weight_rs.at[depth],
                device_id={"chan": chan_of(1 - y_lo, z, which), "seq": seq_to},
                device_id_type=MESH,
            ).start()
        return carry

    lax.fori_loop(0, 8, send_weight, 0)

    local_done(4)
    local_done(5)
    local_done(6)

    def wait_product(peer, carry):
        arrive(prod_recv.at[peer], prod_rs.at[peer])
        return carry

    lax.fori_loop(0, SEQ, wait_product, 0)

    def forward(step, carry):
        rows = pl.ds(pl.multiple_of(step * 256, 256), 256)
        values = prod_recv[...].reshape(512, LANES)
        real = dot(long_v[0, rows, pl.ds(0, 512)], values)
        imag = dot(long_v[1, rows, pl.ds(0, 512)], values)
        tw_cos = twist_v[0, rows, :]
        tw_sin = twist_v[1, rows, :]
        both = jnp.concatenate(
            [
                (real * tw_cos + imag * tw_sin).astype(BF),
                (imag * tw_cos - real * tw_sin).astype(BF),
            ],
            axis=1,
        )
        field[rows, :] = dot(both, short_v[0])
        return carry

    lax.fori_loop(0, 4, forward, 0)

    total[...] = jnp.zeros_like(total)

    def backward(step, carry):
        near = step % 4
        peer = ((y_hi + step // 4) % 2) * 4 + (x + near + near // 2 - 2 * (near // 3)) % 4
        arrive(filt_recv.at[peer], filt_rs.at[peer])
        rows = pl.ds(pl.multiple_of(peer * 128, 128), 128)
        real = field[rows, pl.ds(0, LANES)]
        imag = field[rows, pl.ds(LANES, LANES)]
        filt_real = filt_recv[peer, 0].astype(F32)
        filt_imag = filt_recv[peer, 1].astype(F32)
        both = jnp.concatenate(
            [
                (real * filt_real - imag * filt_imag).astype(BF),
                (real * filt_imag + imag * filt_real).astype(BF),
            ],
            axis=1,
        )
        mixed = dot(both, short_v[1])
        real = mixed[:, :LANES]
        imag = mixed[:, LANES:]
        tw_cos = twist_v[0, rows, :]
        tw_sin = twist_v[1, rows, :]
        turned = jnp.concatenate(
            [
                (real * tw_cos - imag * tw_sin).astype(BF),
                (imag * tw_cos + real * tw_sin).astype(BF),
            ],
            axis=0,
        )
        table = jnp.concatenate(
            [long_v[0, pl.ds(0, 512), rows], long_v[1, pl.ds(0, 512), rows]], axis=1
        )
        total[...] += dot(table, turned)
        return carry

    lax.fori_loop(0, SEQ, backward, 0)
    conv_send[...] = (total[...] * (1.0 / TOTAL)).astype(BF).reshape(SEQ, 64, LANES)
    spread(conv_send, conv_recv, conv_ss, conv_rs)

    local_done(7)

    def wait_conv(peer, carry):
        arrive(conv_recv.at[peer], conv_rs.at[peer])
        return carry

    lax.fori_loop(0, SEQ, wait_conv, 0)
    for tile in range(2):
        block = jnp.concatenate(
            [
                jnp.concatenate(
                    [conv_recv[4 * tile + owner, :, pl.ds(group * 128, 128)] for owner in range(4)],
                    axis=1,
                )
                for group in range(4)
            ],
            axis=0,
        )
        moved = dot(block, moves_v[2]).astype(BF)
        for group in range(4):
            for b in range(4):
                sorted_v[4 * group + b, :, pl.ds(tile * 128, 128)] = moved[
                    group * 64 : (group + 1) * 64, b * 128 : (b + 1) * 128
                ]
    for half in range(2):
        rows = pl.ds(half * 512, 512)
        block = sorted_v[:, pl.ds(half * 32, 32), :].reshape(512, 256)
        conv = dot(moves_v[1], block)
        gated[rows, pl.ds(0, 256)] = (query_v[rows, :].astype(F32) * conv).astype(BF)

    def part(quarter, slot):
        return gated.at[pl.ds(quarter * QUARTER, QUARTER), pl.ds(slot * 256, 256)]

    def gate_copy(kind, quarter, source, target, device):
        return pltpu.make_async_remote_copy(
            part(quarter, source),
            part(quarter, target),
            gate_ss.at[kind, quarter],
            gate_rs.at[kind, quarter],
            device_id=device,
            device_id_type=MESH,
        )

    for quarter in ORDER_OF_QUARTERS:
        gate_copy(0, quarter, 0, 2, across).start()
        gate_copy(1, quarter, 0, 1, sibling).start()

    def wait_weight(depth, carry):
        arrive(weights.at[depth], weight_rs.at[depth])
        return carry

    lax.fori_loop(0, 8, wait_weight, 0)

    def stream(quarter):
        return (quarter // 2, quarter % 2)

    def block_at(quarter, step):
        if quarter // 2 == 0:
            return (z + 15 - step) % 8
        return (z + 1 + step) % 8

    def term(quarter, step):
        rows = pl.ds(quarter * QUARTER, QUARTER)
        return dot(gated[rows, :], weights[block_at(quarter, step)])

    def ring_copy(quarter, step):
        way, sub = stream(quarter)
        return pltpu.make_async_remote_copy(
            ring_send.at[way, sub, step],
            ring_recv.at[way, sub, step],
            ring_ss.at[way, sub, step],
            ring_rs.at[way, sub, step],
            device_id=up if way == 0 else down,
            device_id_type=MESH,
        )

    for quarter in ORDER_OF_QUARTERS:
        way, sub = stream(quarter)
        arrive(part(quarter, 2), gate_rs.at[0, quarter])
        gate_copy(2, quarter, 2, 3, sibling).start()
        arrive(part(quarter, 1), gate_rs.at[1, quarter])
        arrive(part(quarter, 3), gate_rs.at[2, quarter])
        ring_send[way, sub, 0] = term(quarter, 0).astype(BF)
        ring_copy(quarter, 0).start()

    def ring_step(step, carry):
        for quarter in ORDER_OF_QUARTERS:
            way, sub = stream(quarter)
            own = term(quarter, step)
            ring_copy(quarter, step - 1).wait_recv()
            ring_send[way, sub, step] = (own + ring_recv[way, sub, step - 1].astype(F32)).astype(BF)
            ring_copy(quarter, step).start()
        return carry

    lax.fori_loop(1, 7, ring_step, 0)
    for quarter in ORDER_OF_QUARTERS:
        way, sub = stream(quarter)
        own = term(quarter, 7)
        ring_copy(quarter, 6).wait_recv()
        result = own + ring_recv[way, sub, 6].astype(F32)
        out[:, pl.ds(quarter * QUARTER, QUARTER)] = result.T.astype(BF)

    spread_done(prod_send, prod_ss)
    spread_done(filt_send, filt_ss)
    spread_done(conv_send, conv_ss)
    arrive(weights.at[pl.ds(0, 6)], weight_ss)
    for quarter in ORDER_OF_QUARTERS:
        way, sub = stream(quarter)
        gate_copy(0, quarter, 0, 2, across).wait_send()
        gate_copy(1, quarter, 0, 1, sibling).wait_send()
        gate_copy(2, quarter, 2, 3, sibling).wait_send()

        def sent(step, carry):
            ring_copy(quarter, step).wait_send()
            return carry

        lax.fori_loop(0, 7, sent, 0)


def body(query_input, key_input, value_input, filter_spectrum, out_weight):
    moves, long_table, twist, short_table = make_tables()
    filt = filter_spectrum.transpose(2, 1, 0, 3)
    anywhere = pl.BlockSpec(memory_space=pl.ANY)
    dma = pltpu.SemaphoreType.DMA
    return pl.pallas_call(
        kernel,
        out_shape=jax.ShapeDtypeStruct((256, 1024), BF),
        in_specs=[anywhere] * 9,
        out_specs=pl.BlockSpec(memory_space=pltpu.VMEM),
        scratch_shapes=[
            pltpu.VMEM((1024, 256), BF),
            pltpu.VMEM((1024, 256), BF),
            pltpu.VMEM((1024, 256), BF),
            pltpu.VMEM((2, SHORT, 128, 256), BF),
            pltpu.VMEM((3, 512, 512), BF),
            pltpu.VMEM((2, ORDER, ORDER), BF),
            pltpu.VMEM((2, ORDER, LANES), F32),
            pltpu.VMEM((2, 2 * LANES, 2 * LANES), BF),
            pltpu.VMEM((SHORT, 64, 256), BF),
            pltpu.VMEM((SEQ, 64, LANES), BF),
            pltpu.VMEM((SEQ, 64, LANES), BF),
            pltpu.VMEM((SEQ, 2, 128, LANES), BF),
            pltpu.VMEM((SEQ, 2, 128, LANES), BF),
            pltpu.VMEM((ORDER, 2 * LANES), F32),
            pltpu.VMEM((512, LANES), F32),
            pltpu.VMEM((SEQ, 64, LANES), BF),
            pltpu.VMEM((SEQ, 64, LANES), BF),
            pltpu.VMEM((1024, 1024), BF),
            pltpu.VMEM((8, 1024, 256), BF),
            pltpu.VMEM((2, 2, 7, QUARTER, 256), BF),
            pltpu.VMEM((2, 2, 7, QUARTER, 256), BF),
            dma((8,)),
            dma((SEQ,)),
            dma((SEQ,)),
            dma((SEQ,)),
            dma((SEQ,)),
            dma((SEQ,)),
            dma((SEQ,)),
            dma,
            dma((8,)),
            dma((3, 4)),
            dma((3, 4)),
            dma((2, 2, 7)),
            dma((2, 2, 7)),
        ],
        compiler_params=pltpu.CompilerParams(
            collective_id=0, has_side_effects=True, vmem_limit_bytes=58 * 2**20
        ),
        name="hyena",
    )(
        query_input,
        key_input,
        value_input,
        filt,
        out_weight,
        jnp.asarray(moves),
        jnp.asarray(long_table),
        jnp.asarray(twist),
        jnp.asarray(short_table),
    )


def solution(mesh):
    in_specs = (
        P("seq", "chan"),
        P("seq", "chan"),
        P("seq", "chan"),
        P("seq", None, None, "chan"),
        P("chan", None),
    )
    return jax.shard_map(
        body, mesh=mesh, in_specs=in_specs, out_specs=P("chan", "seq"), check_vma=False
    )
```

```python
import functools
import math

import jax
import jax.numpy as jnp
import ml_dtypes
import numpy as np
from jax import lax
from jax.experimental import pallas as pl
from jax.experimental.pallas import tpu as pltpu
from jax.sharding import PartitionSpec as P

BF = jnp.bfloat16
F32 = jnp.float32
ORDER = 1024
SHORT = 16
TOTAL = ORDER * SHORT
SEQ = 8
SUB = 32
LANES = SHORT * SUB
MESH = pl.DeviceIdType.MESH
WAVES = 4
WAVE_ROWS = ORDER // SEQ // WAVES
STREAMS = 4
PIECE = 512 // STREAMS
PIECES = tuple(way * STREAMS + sub for sub in range(STREAMS) for way in range(2))


def make_tables():
    step = np.arange(ORDER)
    angle = 2.0 * math.pi / ORDER * (np.outer(step, step) % ORDER)
    order = step.reshape(SEQ, WAVES, WAVE_ROWS).transpose(1, 0, 2).ravel()
    long = np.stack([np.cos(angle), -np.sin(angle)])
    long_rows = long[:, order, : ORDER // 2]
    long_cols = long[:, : ORDER // 2, order]
    short = np.arange(SHORT)
    angle = 2.0 * math.pi / SHORT * (np.outer(short, short) % SHORT)
    eye = np.eye(SUB)
    short_cos = np.kron(np.cos(angle), eye)
    short_sin = np.kron(np.sin(angle), eye)
    forth = np.block([[short_cos, -short_sin], [short_sin, short_cos]])
    back = np.block([[short_cos, short_sin], [-short_sin, short_cos]])
    angle = 2.0 * math.pi / TOTAL * np.outer(step, short)[order]
    twist_cos = np.repeat(np.cos(angle), SUB, axis=1)
    twist_sin = np.repeat(np.sin(angle), SUB, axis=1)
    rows = np.zeros((512, 512))
    first, second = np.meshgrid(np.arange(32), np.arange(16), indexing="ij")
    rows[(second * 32 + first).ravel(), (first * 16 + second).ravel()] = 1.0
    filt_rows = np.zeros((512, 512))
    first, second, part = np.meshgrid(
        np.arange(16), np.arange(16), np.arange(2), indexing="ij"
    )
    filt_rows[
        (part * 256 + second * 16 + first).ravel(), (first * 32 + second * 2 + part).ravel()
    ] = 1.0
    lanes = np.zeros((512, 512))
    outer, inner, chan = np.meshgrid(np.arange(4), np.arange(4), np.arange(32), indexing="ij")
    lanes[
        (outer * 128 + inner * 32 + chan).ravel(), (inner * 128 + outer * 32 + chan).ravel()
    ] = 1.0

    def half(array):
        return array.astype(np.float32).astype(ml_dtypes.bfloat16)

    return (
        half(np.stack([rows, rows.T, lanes, filt_rows])),
        half(long_rows),
        half(long_cols),
        np.stack([twist_cos, twist_sin]).astype(np.float32),
        half(np.stack([forth, back])),
    )


def dot(left, right):
    return jnp.dot(left, right, preferred_element_type=F32)


def arrive(ref, sem):
    pltpu.make_async_copy(ref, ref, sem).wait()


def kernel(
    query,
    key,
    value,
    filt,
    weight,
    moves,
    rows_table,
    cols_table,
    twist,
    short_table,
    out,
    query_v,
    key_v,
    value_v,
    filt_v,
    moves_v,
    rows_v,
    cols_v,
    twist_v,
    short_v,
    sorted_v,
    filt_sorted,
    prod_send,
    prod_recv,
    filt_send,
    filt_recv,
    field,
    total,
    conv_send,
    conv_recv,
    gated,
    weights,
    ring_send,
    ring_recv,
    local_sem,
    prod_ss,
    prod_rs,
    filt_ss,
    filt_rs,
    conv_ss,
    conv_rs,
    weight_ss,
    weight_rs,
    gate_ss,
    gate_rs,
    ring_ss,
    ring_rs,
):
    chan = lax.axis_index("chan")
    me = lax.axis_index("seq")
    y_lo, z, core = chan // 16, (chan // 2) % 8, chan % 2
    y_hi, x = me // 4, me % 4

    def chan_of(low, depth, which):
        return (low * 8 + depth) * 2 + which

    sibling = {"chan": chan_of(y_lo, z, 1 - core), "seq": me}
    across = {"chan": chan_of(1 - y_lo, z, core), "seq": me}
    far = (1 - y_hi) * 4 + x
    z_up = (z + 1) % 8
    z_down = (z + 7) % 8
    up = {"chan": chan_of(y_lo, z_up, core), "seq": me}
    down = {"chan": chan_of(y_lo, z_down, core), "seq": me}

    local = [
        (key, key_v),
        (value, value_v),
        (moves, moves_v),
        (filt, filt_v),
        (rows_table, rows_v),
        (twist, twist_v),
        (short_table, short_v),
        (cols_table, cols_v),
        (query, query_v),
    ]

    def local_start(*places):
        for at in places:
            pltpu.make_async_copy(local[at][0], local[at][1], local_sem.at[at]).start()

    def local_done(*places):
        for at in places:
            pltpu.make_async_copy(local[at][0], local[at][1], local_sem.at[at]).wait()

    local_start(0, 1, 2, 3)

    barrier = pltpu.get_barrier_semaphore()

    def greet(step, carry):
        peer = (me + step) % SEQ
        pl.semaphore_signal(barrier, 1, device_id={"chan": chan, "seq": peer}, device_id_type=MESH)
        return carry

    lax.fori_loop(1, SEQ, greet, 0)
    for peer in (
        sibling,
        up,
        down,
        across,
        {"chan": chan_of(1 - y_lo, z, 1 - core), "seq": me},
        {"chan": chan_of(1 - y_lo, z, core), "seq": far},
        {"chan": chan_of(1 - y_lo, z, 1 - core), "seq": far},
    ):
        pl.semaphore_signal(barrier, 1, device_id=peer, device_id_type=MESH)

    pl.semaphore_wait(barrier, SEQ - 1 + 7)

    def weight_block(low, depth, which):
        at = pl.multiple_of(chan_of(low, depth, which) * 256, 256)
        return weight.at[:, pl.ds(at, 256)]

    def send_weight_near(depth):
        pltpu.make_async_copy(
            weight_block(y_lo, depth, core), weights.at[depth, pl.ds(0, 256), :], weight_rs.at[depth]
        ).start()
        pltpu.make_async_remote_copy(
            weight_block(y_lo, depth, 1 - core),
            weights.at[depth, pl.ds(256, 256), :],
            weight_ss,
            weight_rs.at[depth],
            device_id=sibling,
            device_id_type=MESH,
        ).start()

    def send_weight_across(depth, seq_to):
        for slot, which in ((2, core), (3, 1 - core)):
            pltpu.make_async_remote_copy(
                weight_block(1 - y_lo, depth, which),
                weights.at[depth, pl.ds(slot * 256, 256), :],
                weight_ss,
                weight_rs.at[depth],
                device_id={"chan": chan_of(1 - y_lo, z, which), "seq": seq_to},
                device_id_type=MESH,
            ).start()

    send_weight_across(z_up, me)
    send_weight_across(z_down, far)

    local_done(0, 1, 2)
    for half in range(2):
        rows = pl.ds(half * 512, 512)
        product = (key_v[rows, :].astype(F32) * value_v[rows, :].astype(F32)).astype(BF)
        moved = dot(moves_v[0], product).astype(BF)
        sorted_v[:, pl.ds(half * 32, 32), :] = moved.reshape(SHORT, 32, 256)
    for tile in range(2):
        block = jnp.concatenate(
            [
                jnp.concatenate(
                    [sorted_v[4 * group + b, :, pl.ds(tile * 128, 128)] for b in range(4)], axis=1
                )
                for group in range(4)
            ],
            axis=0,
        )
        moved = dot(block, moves_v[2]).astype(BF)
        for owner in range(4):
            for group in range(4):
                prod_send[4 * tile + owner, :, pl.ds(group * 128, 128)] = moved[
                    group * 64 : (group + 1) * 64, owner * 128 : (owner + 1) * 128
                ]

    def spread(send, recv, ss, rs):
        def one(step, carry):
            peer = (me + step) % SEQ
            pltpu.make_async_remote_copy(
                send.at[peer],
                recv.at[me],
                ss.at[peer],
                rs.at[me],
                device_id={"chan": chan, "seq": peer},
                device_id_type=MESH,
            ).start()
            return carry

        lax.fori_loop(1, SEQ, one, 0)
        pltpu.make_async_copy(send.at[me], recv.at[me], rs.at[me]).start()

    def spread_done(send, ss):
        def one(step, carry):
            peer = (me + step) % SEQ
            arrive(send.at[peer], ss.at[peer])
            return carry

        lax.fori_loop(1, SEQ, one, 0)

    spread(prod_send, prod_recv, prod_ss, prod_rs)

    local_start(4, 5, 6)
    local_done(3)

    def filt_copy(wave, peer):
        return pltpu.make_async_remote_copy(
            filt_send.at[wave, peer],
            filt_recv.at[wave, me],
            filt_ss.at[wave],
            filt_rs.at[wave],
            device_id={"chan": chan, "seq": peer},
            device_id_type=MESH,
        )

    def send_filter(wave, carry):
        for at in range(2):
            block = filt_v[pl.ds((2 * wave + at) * 16, 16)].reshape(512, 256)
            moved = dot(moves_v[3], block).astype(BF)
            filt_sorted[:, :, pl.ds(at * 16, 16), :] = moved.reshape(2, SHORT, 16, 256)
        for tile in range(2):
            block = jnp.concatenate(
                [
                    jnp.concatenate(
                        [
                            filt_sorted[at, 4 * group + b, :, pl.ds(tile * 128, 128)]
                            for b in range(4)
                        ],
                        axis=1,
                    )
                    for at in range(2)
                    for group in range(4)
                ],
                axis=0,
            )
            moved = dot(block, moves_v[2]).astype(BF)
            for owner in range(4):
                for at in range(2):
                    for group in range(4):
                        first = (at * 4 + group) * WAVE_ROWS
                        filt_send[
                            wave, 4 * tile + owner, at, :, pl.ds(group * 128, 128)
                        ] = moved[first : first + WAVE_ROWS, owner * 128 : (owner + 1) * 128]

        def one(step, carry):
            filt_copy(wave, (me + step) % SEQ).start()
            return carry

        lax.fori_loop(1, SEQ, one, 0)
        pltpu.make_async_copy(
            filt_send.at[wave, me], filt_recv.at[wave, me], filt_rs.at[wave]
        ).start()
        return carry

    lax.fori_loop(0, WAVES, send_filter, 0)
    local_start(7, 8)

    def near_weights(depth, carry):
        send_weight_near(depth)
        return carry

    lax.fori_loop(0, 8, near_weights, 0)

    local_done(4, 5, 6)

    def wait_product(peer, carry):
        arrive(prod_recv.at[peer], prod_rs.at[peer])
        return carry

    lax.fori_loop(0, SEQ, wait_product, 0)

    def forward(step, carry):
        rows = pl.ds(pl.multiple_of(step * 256, 256), 256)
        values = prod_recv[...].reshape(512, LANES)
        real = dot(rows_v[0, rows, :], values)
        imag = dot(rows_v[1, rows, :], values)
        tw_cos = twist_v[0, rows, :]
        tw_sin = twist_v[1, rows, :]
        both = jnp.concatenate(
            [
                (real * tw_cos + imag * tw_sin).astype(BF),
                (imag * tw_cos - real * tw_sin).astype(BF),
            ],
            axis=1,
        )
        field[rows, :] = dot(both, short_v[0])
        return carry

    lax.fori_loop(0, 4, forward, 0)

    total[...] = jnp.zeros_like(total)
    local_done(7)

    def backward(wave, carry):
        arrive(filt_recv.at[wave], filt_rs.at[wave])
        rows = pl.ds(pl.multiple_of(wave * 256, 256), 256)
        real = field[rows, pl.ds(0, LANES)]
        imag = field[rows, pl.ds(LANES, LANES)]
        filt_real = filt_recv[wave, :, 0].reshape(256, LANES).astype(F32)
        filt_imag = filt_recv[wave, :, 1].reshape(256, LANES).astype(F32)
        both = jnp.concatenate(
            [
                (real * filt_real - imag * filt_imag).astype(BF),
                (real * filt_imag + imag * filt_real).astype(BF),
            ],
            axis=1,
        )
        mixed = dot(both, short_v[1])
        real = mixed[:, :LANES]
        imag = mixed[:, LANES:]
        tw_cos = twist_v[0, rows, :]
        tw_sin = twist_v[1, rows, :]
        turned = jnp.concatenate(
            [
                (real * tw_cos - imag * tw_sin).astype(BF),
                (imag * tw_cos + real * tw_sin).astype(BF),
            ],
            axis=0,
        )
        table = jnp.concatenate([cols_v[0, :, rows], cols_v[1, :, rows]], axis=1)
        total[...] += dot(table, turned)
        return carry

    lax.fori_loop(0, WAVES, backward, 0)
    conv_send[...] = (total[...] * (1.0 / TOTAL)).astype(BF).reshape(SEQ, 64, LANES)
    spread(conv_send, conv_recv, conv_ss, conv_rs)

    local_done(8)

    def wait_conv(peer, carry):
        arrive(conv_recv.at[peer], conv_rs.at[peer])
        return carry

    lax.fori_loop(0, SEQ, wait_conv, 0)
    for tile in range(2):
        block = jnp.concatenate(
            [
                jnp.concatenate(
                    [conv_recv[4 * tile + owner, :, pl.ds(group * 128, 128)] for owner in range(4)],
                    axis=1,
                )
                for group in range(4)
            ],
            axis=0,
        )
        moved = dot(block, moves_v[2]).astype(BF)
        for group in range(4):
            for b in range(4):
                sorted_v[4 * group + b, :, pl.ds(tile * 128, 128)] = moved[
                    group * 64 : (group + 1) * 64, b * 128 : (b + 1) * 128
                ]
    for half in range(2):
        rows = pl.ds(half * 512, 512)
        block = sorted_v[:, pl.ds(half * 32, 32), :].reshape(512, 256)
        conv = dot(moves_v[1], block)
        gated[rows, pl.ds(0, 256)] = (query_v[rows, :].astype(F32) * conv).astype(BF)

    def part(piece, slot):
        return gated.at[pl.ds(piece * PIECE, PIECE), pl.ds(slot * 256, 256)]

    def gate_copy(kind, piece, source, target, device):
        return pltpu.make_async_remote_copy(
            part(piece, source),
            part(piece, target),
            gate_ss.at[kind, piece],
            gate_rs.at[kind, piece],
            device_id=device,
            device_id_type=MESH,
        )

    for piece in PIECES:
        gate_copy(0, piece, 0, 2, across).start()
        gate_copy(1, piece, 0, 1, sibling).start()

    send_weight_across((z + 2) % 8, far)
    send_weight_across((z + 6) % 8, far)
    send_weight_across((z + 3) % 8, me)
    send_weight_across((z + 5) % 8, far)
    send_weight_across((z + 4) % 8, me)
    send_weight_across(z, far)

    def wait_weight(depth):
        arrive(weights.at[depth], weight_rs.at[depth])

    def block_at(piece, step):
        if piece // STREAMS == 0:
            return (z + 15 - step) % 8
        return (z + 1 + step) % 8

    def term(piece, step):
        rows = pl.ds(piece * PIECE, PIECE)
        return dot(gated[rows, :], weights[block_at(piece, step)])

    def ring_copy(piece, step):
        return pltpu.make_async_remote_copy(
            ring_send.at[piece, step],
            ring_recv.at[piece, step],
            ring_ss.at[piece, step],
            ring_rs.at[piece, step],
            device_id=up if piece // STREAMS == 0 else down,
            device_id_type=MESH,
        )

    wait_weight(z_up)
    wait_weight(z_down)
    for piece in PIECES:
        arrive(part(piece, 2), gate_rs.at[0, piece])
        gate_copy(2, piece, 2, 3, sibling).start()
        arrive(part(piece, 1), gate_rs.at[1, piece])
        arrive(part(piece, 3), gate_rs.at[2, piece])
        ring_send[piece, 0] = term(piece, 0).astype(BF)
        ring_copy(piece, 0).start()

    def ring_step(step, carry):
        @pl.when(step < 4)
        def _():
            wait_weight((z + 1 + step) % 8)

        @pl.when(step < 3)
        def _():
            wait_weight((z + 7 - step) % 8)

        for piece in PIECES:
            own = term(piece, step)
            ring_copy(piece, step - 1).wait_recv()
            ring_send[piece, step] = (own + ring_recv[piece, step - 1].astype(F32)).astype(BF)
            ring_copy(piece, step).start()
        return carry

    lax.fori_loop(1, 7, ring_step, 0)
    wait_weight(z)
    for piece in PIECES:
        own = term(piece, 7)
        ring_copy(piece, 6).wait_recv()
        result = own + ring_recv[piece, 6].astype(F32)
        out[pl.ds(piece * PIECE, PIECE), :] = result.astype(BF)

    spread_done(prod_send, prod_ss)
    spread_done(conv_send, conv_ss)

    def filter_sent(wave, carry):
        arrive(filt_send.at[wave, pl.ds(0, SEQ - 1)], filt_ss.at[wave])
        return carry

    lax.fori_loop(0, WAVES, filter_sent, 0)
    arrive(weights.at[pl.ds(0, 6)], weight_ss)
    for piece in PIECES:
        gate_copy(0, piece, 0, 2, across).wait_send()
        gate_copy(1, piece, 0, 1, sibling).wait_send()
        gate_copy(2, piece, 2, 3, sibling).wait_send()

        def sent(step, carry):
            ring_copy(piece, step).wait_send()
            return carry

        lax.fori_loop(0, 7, sent, 0)


def body(query_input, key_input, value_input, filter_spectrum, out_weight):
    moves, rows_table, cols_table, twist, short_table = make_tables()
    anywhere = pl.BlockSpec(memory_space=pl.ANY)
    dma = pltpu.SemaphoreType.DMA
    mixed = pl.pallas_call(
        kernel,
        out_shape=pltpu.VMEM((1024, 256), BF),
        in_specs=[anywhere] * 10,
        out_specs=pl.BlockSpec(memory_space=pltpu.VMEM),
        scratch_shapes=[
            pltpu.VMEM((1024, 256), BF),
            pltpu.VMEM((1024, 256), BF),
            pltpu.VMEM((1024, 256), BF),
            pltpu.VMEM((128, SHORT, 2, 256), BF),
            pltpu.VMEM((4, 512, 512), BF),
            pltpu.VMEM((2, ORDER, ORDER // 2), BF),
            pltpu.VMEM((2, ORDER // 2, ORDER), BF),
            pltpu.VMEM((2, ORDER, LANES), F32),
            pltpu.VMEM((2, 2 * LANES, 2 * LANES), BF),
            pltpu.VMEM((SHORT, 64, 256), BF),
            pltpu.VMEM((2, SHORT, WAVE_ROWS, 256), BF),
            pltpu.VMEM((SEQ, 64, LANES), BF),
            pltpu.VMEM((SEQ, 64, LANES), BF),
            pltpu.VMEM((WAVES, SEQ, 2, WAVE_ROWS, LANES), BF),
            pltpu.VMEM((WAVES, SEQ, 2, WAVE_ROWS, LANES), BF),
            pltpu.VMEM((ORDER, 2 * LANES), F32),
            pltpu.VMEM((512, LANES), F32),
            pltpu.VMEM((SEQ, 64, LANES), BF),
            pltpu.VMEM((SEQ, 64, LANES), BF),
            pltpu.VMEM((1024, 1024), BF),
            pltpu.VMEM((8, 1024, 256), BF),
            pltpu.VMEM((2 * STREAMS, 7, PIECE, 256), BF),
            pltpu.VMEM((2 * STREAMS, 7, PIECE, 256), BF),
            dma((9,)),
            dma((SEQ,)),
            dma((SEQ,)),
            dma((WAVES,)),
            dma((WAVES,)),
            dma((SEQ,)),
            dma((SEQ,)),
            dma,
            dma((8,)),
            dma((3, 2 * STREAMS)),
            dma((3, 2 * STREAMS)),
            dma((2 * STREAMS, 7)),
            dma((2 * STREAMS, 7)),
        ],
        compiler_params=pltpu.CompilerParams(
            collective_id=0, has_side_effects=True, vmem_limit_bytes=58 * 2**20
        ),
        name="hyena",
    )(
        query_input,
        key_input,
        value_input,
        filter_spectrum,
        out_weight,
        jnp.asarray(moves),
        jnp.asarray(rows_table),
        jnp.asarray(cols_table),
        jnp.asarray(twist),
        jnp.asarray(short_table),
    )
    return mixed.T


def solution(mesh):
    in_specs = (
        P("seq", "chan"),
        P("seq", "chan"),
        P("seq", "chan"),
        P("seq", None, None, "chan"),
        P("chan", None),
    )
    return jax.shard_map(
        body, mesh=mesh, in_specs=in_specs, out_specs=P("chan", "seq"), check_vma=False
    )
```

```python
import functools
import math

import jax
import jax.numpy as jnp
import ml_dtypes
import numpy as np
from jax import lax
from jax.experimental import pallas as pl
from jax.experimental.pallas import tpu as pltpu
from jax.sharding import PartitionSpec as P

BF = jnp.bfloat16
F32 = jnp.float32
ORDER = 1024
SHORT = 16
TOTAL = ORDER * SHORT
SEQ = 8
SHARES = 2
SUB = 16
LANES = SHORT * SUB
MESH = pl.DeviceIdType.MESH
WAVES = 4
WAVE_ROWS = ORDER // SEQ // WAVES
STREAMS = 4
PIECE = 512 // STREAMS


def make_tables():
    step = np.arange(ORDER)
    angle = 2.0 * math.pi / ORDER * (np.outer(step, step) % ORDER)
    order = step.reshape(SEQ, WAVES, WAVE_ROWS).transpose(1, 0, 2).ravel()
    long = np.stack([np.cos(angle), -np.sin(angle)])
    long_rows = long[:, order, : ORDER // 2]
    long_cols = long[:, : ORDER // 2, order]
    short = np.arange(SHORT)
    angle = 2.0 * math.pi / SHORT * (np.outer(short, short) % SHORT)
    eye = np.eye(SUB)
    short_cos = np.kron(np.cos(angle), eye)
    short_sin = np.kron(np.sin(angle), eye)
    forth = np.block([[short_cos, -short_sin], [short_sin, short_cos]])
    back = np.block([[short_cos, short_sin], [-short_sin, short_cos]])
    angle = 2.0 * math.pi / TOTAL * np.outer(step, short)[order]
    twist_cos = np.repeat(np.cos(angle), SUB, axis=1)
    twist_sin = np.repeat(np.sin(angle), SUB, axis=1)
    rows = np.zeros((512, 512))
    first, second = np.meshgrid(np.arange(32), np.arange(16), indexing="ij")
    rows[(second * 32 + first).ravel(), (first * 16 + second).ravel()] = 1.0
    filt_rows = np.zeros((512, 512))
    first, second, part = np.meshgrid(
        np.arange(16), np.arange(16), np.arange(2), indexing="ij"
    )
    filt_rows[
        (part * 256 + second * 16 + first).ravel(), (first * 32 + second * 2 + part).ravel()
    ] = 1.0
    lanes = np.zeros((1024, 1024))
    outer, inner, chan = np.meshgrid(np.arange(8), np.arange(8), np.arange(16), indexing="ij")
    lanes[
        (outer * 128 + inner * 16 + chan).ravel(), (inner * 128 + outer * 16 + chan).ravel()
    ] = 1.0

    def half(array):
        return array.astype(np.float32).astype(ml_dtypes.bfloat16)

    return (
        half(np.stack([rows, rows.T, filt_rows])),
        half(lanes),
        half(long_rows),
        half(long_cols),
        np.stack([twist_cos, twist_sin]).astype(np.float32),
        half(np.stack([forth, back])),
    )


def dot(left, right):
    return jnp.dot(left, right, preferred_element_type=F32)


def arrive(ref, sem):
    pltpu.make_async_copy(ref, ref, sem).wait()


def kernel(
    query,
    key,
    value,
    filt,
    weight,
    moves,
    lanes_table,
    rows_table,
    cols_table,
    twist,
    short_table,
    out,
    query_v,
    key_v,
    value_v,
    filt_v,
    moves_v,
    lanes_v,
    rows_v,
    cols_v,
    twist_v,
    short_v,
    sorted_v,
    filt_sorted,
    prod_send,
    prod_recv,
    filt_send,
    filt_recv,
    field,
    total,
    conv_send,
    conv_recv,
    gated,
    weights,
    ring_send,
    ring_recv,
    local_sem,
    prod_ss,
    prod_rs,
    filt_ss,
    filt_rs,
    conv_ss,
    conv_rs,
    weight_ss,
    weight_rs,
    share_rs,
    gate_ss,
    gate_rs,
    ring_ss,
    ring_rs,
):
    chan = lax.axis_index("chan")
    me = lax.axis_index("seq")
    y_lo, z, core = chan // 16, (chan // 2) % 8, chan % 2
    y_hi, x = me // 4, me % 4

    def chan_of(low, depth, which):
        return (low * 8 + depth) * 2 + which

    sibling = {"chan": chan_of(y_lo, z, 1 - core), "seq": me}
    across = {"chan": chan_of(1 - y_lo, z, core), "seq": me}
    far = (1 - y_hi) * 4 + x
    z_up = (z + 1) % 8
    z_down = (z + 7) % 8

    local = [
        (key, key_v),
        (value, value_v),
        (moves, moves_v),
        (lanes_table, lanes_v),
        (filt, filt_v),
        (rows_table, rows_v),
        (twist, twist_v),
        (short_table, short_v),
        (cols_table, cols_v),
        (query, query_v),
    ]

    def local_start(*places):
        for at in places:
            pltpu.make_async_copy(local[at][0], local[at][1], local_sem.at[at]).start()

    def local_done(*places):
        for at in places:
            pltpu.make_async_copy(local[at][0], local[at][1], local_sem.at[at]).wait()

    local_start(0, 1, 2, 3, 4)

    barrier = pltpu.get_barrier_semaphore()

    def greet(step, carry):
        peer = (me + step) % SEQ
        pl.semaphore_signal(barrier, 1, device_id={"chan": chan, "seq": peer}, device_id_type=MESH)
        return carry

    lax.fori_loop(1, SEQ, greet, 0)
    for peer in (
        sibling,
        {"chan": chan_of(y_lo, z_up, core), "seq": me},
        {"chan": chan_of(y_lo, z_down, core), "seq": me},
        across,
        {"chan": chan_of(1 - y_lo, z, 1 - core), "seq": me},
        {"chan": chan_of(1 - y_lo, z, core), "seq": far},
        {"chan": chan_of(1 - y_lo, z, 1 - core), "seq": far},
    ):
        pl.semaphore_signal(barrier, 1, device_id=peer, device_id_type=MESH)

    pl.semaphore_wait(barrier, SEQ - 1 + 7)

    def weight_block(low, depth, which):
        at = pl.multiple_of(chan_of(low, depth, which) * 256, 256)
        return weight.at[:, pl.ds(at, 256)]

    def send_weight_near(depth):
        pltpu.make_async_copy(
            weight_block(y_lo, depth, core), weights.at[depth, pl.ds(0, 256), :], weight_rs.at[depth]
        ).start()
        pltpu.make_async_remote_copy(
            weight_block(y_lo, depth, 1 - core),
            weights.at[depth, pl.ds(256, 256), :],
            weight_ss,
            weight_rs.at[depth],
            device_id=sibling,
            device_id_type=MESH,
        ).start()

    core_across = (core + x // 2) % 2
    row_across = pl.multiple_of((x % 2) * 128, 128)
    row_shared = pl.multiple_of(512 + x * 128, 128)

    def send_weight_across(step, seq_to):
        depth = (z + step) % 8
        at = pl.multiple_of(chan_of(1 - y_lo, depth, core_across) * 256, 256)
        pltpu.make_async_remote_copy(
            weight.at[pl.ds(row_across, 128), pl.ds(at, 256)],
            weights.at[depth, pl.ds(row_shared, 128), :],
            weight_ss,
            share_rs,
            device_id={"chan": chan_of(1 - y_lo, z, core_across), "seq": seq_to},
            device_id_type=MESH,
        ).start()

    def share_weight(step):
        depth = (z + step) % 8
        shared = weights.at[depth, pl.ds(row_shared, 128), :]
        for peer in (1, 3, 2):
            pltpu.make_async_remote_copy(
                shared,
                shared,
                weight_ss,
                weight_rs.at[depth],
                device_id={"chan": chan, "seq": y_hi * 4 + (x + peer) % 4},
                device_id_type=MESH,
            ).start()

    for step, seq_to in ((1, me), (7, far), (2, far), (6, me), (3, me), (5, far), (4, me), (0, far)):
        send_weight_across(step, seq_to)

    local_done(0, 1, 2)
    for half in range(2):
        rows = pl.ds(half * 512, 512)
        product = (key_v[rows, :].astype(F32) * value_v[rows, :].astype(F32)).astype(BF)
        moved = dot(moves_v[0], product).astype(BF)
        sorted_v[:, pl.ds(half * 32, 32), :] = moved.reshape(SHORT, 32, 256)
    local_done(3)
    for share in range(SHARES):
        block = jnp.concatenate(
            [
                jnp.concatenate(
                    [sorted_v[8 * group + b, :, pl.ds(share * 128, 128)] for b in range(8)], axis=1
                )
                for group in range(2)
            ],
            axis=0,
        )
        moved = dot(block, lanes_v[...]).astype(BF)
        for owner in range(SEQ):
            for group in range(2):
                prod_send[share, owner, :, pl.ds(group * 128, 128)] = moved[
                    group * 64 : (group + 1) * 64, owner * 128 : (owner + 1) * 128
                ]


    def spread(send, recv, ss, rs):
        def one(step, carry):
            peer = (me + step) % SEQ
            pltpu.make_async_remote_copy(
                send.at[peer],
                recv.at[me],
                ss,
                rs,
                device_id={"chan": chan, "seq": peer},
                device_id_type=MESH,
            ).start()
            return carry

        lax.fori_loop(1, SEQ, one, 0)
        pltpu.make_async_copy(send.at[me], recv.at[me], rs).start()

    for share in range(SHARES):
        spread(prod_send.at[share], prod_recv.at[share], prod_ss.at[share], prod_rs.at[share])

    local_start(5, 6, 7)
    local_done(4)

    def send_filter(share, wave):
        block = jnp.concatenate(
            [
                jnp.concatenate(
                    [
                        filt_sorted[wave, at, 8 * group + b, :, pl.ds(share * 128, 128)]
                        for b in range(8)
                    ],
                    axis=1,
                )
                for at in range(2)
                for group in range(2)
            ],
            axis=0,
        )
        moved = dot(block, lanes_v[...]).astype(BF)
        for owner in range(SEQ):
            for at in range(2):
                for group in range(2):
                    first = (at * 2 + group) * WAVE_ROWS
                    filt_send[share, wave, owner, at, :, pl.ds(group * 128, 128)] = moved[
                        first : first + WAVE_ROWS, owner * 128 : (owner + 1) * 128
                    ]
        spread(
            filt_send.at[share, wave],
            filt_recv.at[share, wave],
            filt_ss.at[share, wave],
            filt_rs.at[share, wave],
        )

    def sort_filter(wave, carry):
        for at in range(2):
            block = filt_v[pl.ds((2 * wave + at) * 16, 16)].reshape(512, 256)
            moved = dot(moves_v[2], block).astype(BF)
            filt_sorted[wave, :, :, pl.ds(at * 16, 16), :] = moved.reshape(2, SHORT, 16, 256)
        send_filter(0, wave)
        return carry

    def rest_of_filter(wave, carry):
        send_filter(1, wave)
        return carry

    lax.fori_loop(0, WAVES, sort_filter, 0)
    lax.fori_loop(0, WAVES, rest_of_filter, 0)
    local_start(8, 9)

    def near_weights(depth, carry):
        send_weight_near(depth)
        return carry

    lax.fori_loop(0, 8, near_weights, 0)
    arrive(weights.at[0], share_rs)
    share_weight(1)
    share_weight(7)

    local_done(5, 6, 7)

    def forward(at, carry):
        share, step = at // 4, at % 4

        @pl.when(step == 0)
        def _():
            arrive(prod_recv.at[share], prod_rs.at[share])

        rows = pl.ds(pl.multiple_of(step * 256, 256), 256)
        values = prod_recv[share].reshape(512, LANES)
        real = dot(rows_v[0, rows, :], values)
        imag = dot(rows_v[1, rows, :], values)
        tw_cos = twist_v[0, rows, :]
        tw_sin = twist_v[1, rows, :]
        both = jnp.concatenate(
            [
                (real * tw_cos + imag * tw_sin).astype(BF),
                (imag * tw_cos - real * tw_sin).astype(BF),
            ],
            axis=1,
        )
        field[share, rows, :] = dot(both, short_v[0])
        return carry

    lax.fori_loop(0, SHARES * 4, forward, 0)
    local_done(8)

    def inverse(share):
        total[...] = jnp.zeros_like(total)

        def backward(wave, carry):
            arrive(filt_recv.at[share, wave], filt_rs.at[share, wave])
            rows = pl.ds(pl.multiple_of(wave * 256, 256), 256)
            real = field[share, rows, pl.ds(0, LANES)]
            imag = field[share, rows, pl.ds(LANES, LANES)]
            filt_real = filt_recv[share, wave, :, 0].reshape(256, LANES).astype(F32)
            filt_imag = filt_recv[share, wave, :, 1].reshape(256, LANES).astype(F32)
            both = jnp.concatenate(
                [
                    (real * filt_real - imag * filt_imag).astype(BF),
                    (real * filt_imag + imag * filt_real).astype(BF),
                ],
                axis=1,
            )
            mixed = dot(both, short_v[1])
            real = mixed[:, :LANES]
            imag = mixed[:, LANES:]
            tw_cos = twist_v[0, rows, :]
            tw_sin = twist_v[1, rows, :]
            turned = jnp.concatenate(
                [
                    (real * tw_cos - imag * tw_sin).astype(BF),
                    (imag * tw_cos + real * tw_sin).astype(BF),
                ],
                axis=0,
            )
            table = jnp.concatenate([cols_v[0, :, rows], cols_v[1, :, rows]], axis=1)
            total[...] += dot(table, turned)
            return carry

        lax.fori_loop(0, WAVES, backward, 0)
        conv_send[share] = (total[...] * (1.0 / TOTAL)).astype(BF).reshape(SEQ, 64, LANES)
        spread(conv_send.at[share], conv_recv.at[share], conv_ss.at[share], conv_rs.at[share])

    def rows_of(piece):
        return pl.ds(pl.multiple_of(piece * PIECE, PIECE), PIECE)

    def part(piece, slot, share):
        return gated.at[rows_of(piece), pl.ds(slot * 256 + share * 128, 128)]

    def gate_copy(kind, piece, share, source, target, device):
        return pltpu.make_async_remote_copy(
            part(piece, source, share),
            part(piece, target, share),
            gate_ss.at[kind, share],
            gate_rs.at[kind, share, piece],
            device_id=device,
            device_id_type=MESH,
        )

    def piece_of(at):
        return (at % 2) * STREAMS + at // 2

    def gate(share):
        arrive(conv_recv.at[share], conv_rs.at[share])
        lanes = pl.ds(share * 128, 128)
        block = jnp.concatenate(
            [
                jnp.concatenate(
                    [conv_recv[share, owner, :, pl.ds(group * 128, 128)] for owner in range(SEQ)],
                    axis=1,
                )
                for group in range(2)
            ],
            axis=0,
        )
        moved = dot(block, lanes_v[...]).astype(BF)
        for group in range(2):
            for b in range(8):
                sorted_v[8 * group + b, :, lanes] = moved[
                    group * 64 : (group + 1) * 64, b * 128 : (b + 1) * 128
                ]
        for half in range(2):
            rows = pl.ds(half * 512, 512)
            block = sorted_v[:, pl.ds(half * 32, 32), lanes].reshape(512, 128)
            conv = dot(moves_v[1], block)
            gated[rows, lanes] = (query_v[rows, lanes].astype(F32) * conv).astype(BF)

        def send_gated(at, carry):
            piece = piece_of(at)
            gate_copy(0, piece, share, 0, 2, across).start()
            gate_copy(1, piece, share, 0, 1, sibling).start()
            return carry

        lax.fori_loop(0, 2 * STREAMS, send_gated, 0)

    def pass_on(piece, share):
        arrive(part(piece, 2, share), gate_rs.at[0, share, piece])
        gate_copy(2, piece, share, 2, 3, sibling).start()

    def gate_done(piece, share):
        arrive(part(piece, 1, share), gate_rs.at[1, share, piece])
        arrive(part(piece, 3, share), gate_rs.at[2, share, piece])

    local_done(9)
    inverse(0)
    inverse(1)
    gate(0)
    share_weight(2)
    share_weight(6)

    def pass_first(at, carry):
        pass_on(piece_of(at), 0)
        return carry

    gate(1)
    lax.fori_loop(0, 2 * STREAMS, pass_first, 0)
    for step in (3, 5, 4, 0):
        share_weight(step)

    def wait_weight(step):
        depth = (z + step) % 8
        arrive(weights.at[depth, pl.ds(0, 896), :], weight_rs.at[depth])

    def term(piece, step):
        depth = (z + 7 - step) % 8 if piece // STREAMS == 0 else (z + 1 + step) % 8
        return dot(gated[rows_of(piece), :], weights[depth])

    def ring_copy(piece, step):
        depth = z_up if piece // STREAMS == 0 else z_down
        return pltpu.make_async_remote_copy(
            ring_send.at[piece, step],
            ring_recv.at[piece, step],
            ring_ss.at[piece],
            ring_rs.at[piece, step],
            device_id={"chan": chan_of(y_lo, depth, core), "seq": me},
            device_id_type=MESH,
        )

    wait_weight(1)
    wait_weight(7)
    for sub in range(STREAMS):
        for piece in (sub, sub + STREAMS):
            pass_on(piece, 1)
        for piece in (sub, sub + STREAMS):
            gate_done(piece, 0)
            gate_done(piece, 1)
            ring_send[piece, 0] = term(piece, 0).astype(BF)
            ring_copy(piece, 0).start()

    def ring_step(step, carry):
        @pl.when(step < 4)
        def _():
            wait_weight(1 + step)

        @pl.when(step < 3)
        def _():
            wait_weight(7 - step)

        for sub in range(STREAMS):
            for piece in (sub, sub + STREAMS):
                own = term(piece, step)
                ring_copy(piece, step - 1).wait_recv()
                ring_send[piece, step] = (own + ring_recv[piece, step - 1].astype(F32)).astype(BF)
                ring_copy(piece, step).start()
        return carry

    lax.fori_loop(1, 7, ring_step, 0)
    wait_weight(0)
    for sub in range(STREAMS):
        for piece in (sub, sub + STREAMS):
            own = term(piece, 7)
            ring_copy(piece, 6).wait_recv()
            out[rows_of(piece), :] = (own + ring_recv[piece, 6].astype(F32)).astype(BF)

    for share in range(SHARES):
        arrive(prod_send.at[share, pl.ds(0, SEQ - 1)], prod_ss.at[share])
        arrive(conv_send.at[share, pl.ds(0, SEQ - 1)], conv_ss.at[share])
        for wave in range(WAVES):
            arrive(filt_send.at[share, wave, pl.ds(0, SEQ - 1)], filt_ss.at[share, wave])
        for kind in range(3):
            arrive(gated.at[:, pl.ds(0, 128)], gate_ss.at[kind, share])
    arrive(weights.at[pl.ds(0, 6)], weight_ss)
    for piece in range(2 * STREAMS):
        arrive(ring_send.at[piece], ring_ss.at[piece])


def body(query_input, key_input, value_input, filter_spectrum, out_weight):
    moves, lanes_table, rows_table, cols_table, twist, short_table = make_tables()
    anywhere = pl.BlockSpec(memory_space=pl.ANY)
    dma = pltpu.SemaphoreType.DMA
    mixed = pl.pallas_call(
        kernel,
        out_shape=pltpu.VMEM((1024, 256), BF),
        in_specs=[anywhere] * 11,
        out_specs=pl.BlockSpec(memory_space=pltpu.VMEM),
        scratch_shapes=[
            pltpu.VMEM((1024, 256), BF),
            pltpu.VMEM((1024, 256), BF),
            pltpu.VMEM((1024, 256), BF),
            pltpu.VMEM((128, SHORT, 2, 256), BF),
            pltpu.VMEM((3, 512, 512), BF),
            pltpu.VMEM((1024, 1024), BF),
            pltpu.VMEM((2, ORDER, ORDER // 2), BF),
            pltpu.VMEM((2, ORDER // 2, ORDER), BF),
            pltpu.VMEM((2, ORDER, LANES), F32),
            pltpu.VMEM((2, 2 * LANES, 2 * LANES), BF),
            pltpu.VMEM((SHORT, 64, 256), BF),
            pltpu.VMEM((WAVES, 2, SHORT, WAVE_ROWS, 256), BF),
            pltpu.VMEM((SHARES, SEQ, 64, LANES), BF),
            pltpu.VMEM((SHARES, SEQ, 64, LANES), BF),
            pltpu.VMEM((SHARES, WAVES, SEQ, 2, WAVE_ROWS, LANES), BF),
            pltpu.VMEM((SHARES, WAVES, SEQ, 2, WAVE_ROWS, LANES), BF),
            pltpu.VMEM((SHARES, ORDER, 2 * LANES), F32),
            pltpu.VMEM((512, LANES), F32),
            pltpu.VMEM((SHARES, SEQ, 64, LANES), BF),
            pltpu.VMEM((SHARES, SEQ, 64, LANES), BF),
            pltpu.VMEM((1024, 1024), BF),
            pltpu.VMEM((8, 1024, 256), BF),
            pltpu.VMEM((2 * STREAMS, 7, PIECE, 256), BF),
            pltpu.VMEM((2 * STREAMS, 7, PIECE, 256), BF),
            dma((10,)),
            dma((SHARES,)),
            dma((SHARES,)),
            dma((SHARES, WAVES)),
            dma((SHARES, WAVES)),
            dma((SHARES,)),
            dma((SHARES,)),
            dma,
            dma((8,)),
            dma,
            dma((3, SHARES)),
            dma((3, SHARES, 2 * STREAMS)),
            dma((2 * STREAMS,)),
            dma((2 * STREAMS, 7)),
        ],
        compiler_params=pltpu.CompilerParams(
            collective_id=0, has_side_effects=True, vmem_limit_bytes=58 * 2**20
        ),
        name="hyena",
    )(
        query_input,
        key_input,
        value_input,
        filter_spectrum,
        out_weight,
        jnp.asarray(moves),
        jnp.asarray(lanes_table),
        jnp.asarray(rows_table),
        jnp.asarray(cols_table),
        jnp.asarray(twist),
        jnp.asarray(short_table),
    )
    return mixed.T


def solution(mesh):
    in_specs = (
        P("seq", "chan"),
        P("seq", "chan"),
        P("seq", "chan"),
        P("seq", None, None, "chan"),
        P("chan", None),
    )
    return jax.shard_map(
        body, mesh=mesh, in_specs=in_specs, out_specs=P("chan", "seq"), check_vma=False
    )
```

```python
import functools
import math

import jax
import jax.numpy as jnp
import ml_dtypes
import numpy as np
from jax import lax
from jax.experimental import pallas as pl
from jax.experimental.pallas import tpu as pltpu
from jax.sharding import PartitionSpec as P

BF = jnp.bfloat16
F32 = jnp.float32
ORDER = 1024
SHORT = 16
TOTAL = ORDER * SHORT
SEQ = 8
SHARES = 2
SUB = 16
LANES = SHORT * SUB
MESH = pl.DeviceIdType.MESH
WAVES = 4
WAVE_ROWS = ORDER // SEQ // WAVES
STREAMS = 4
PIECE = 512 // STREAMS


def make_tables():
    step = np.arange(ORDER)
    angle = 2.0 * math.pi / ORDER * (np.outer(step, step) % ORDER)
    order = step.reshape(SEQ, WAVES, WAVE_ROWS).transpose(1, 0, 2).ravel()
    long = np.stack([np.cos(angle), -np.sin(angle)])
    long_rows = long[:, order, : ORDER // 2]
    long_cols = long[:, : ORDER // 2, order]
    short = np.arange(SHORT)
    angle = 2.0 * math.pi / SHORT * (np.outer(short, short) % SHORT)
    eye = np.eye(SUB)
    short_cos = np.kron(np.cos(angle), eye)
    short_sin = np.kron(np.sin(angle), eye)
    forth = np.block([[short_cos, -short_sin], [short_sin, short_cos]])
    back = np.block([[short_cos, short_sin], [-short_sin, short_cos]])
    angle = 2.0 * math.pi / TOTAL * np.outer(step, short)[order]
    twist_cos = np.repeat(np.cos(angle), SUB, axis=1)
    twist_sin = np.repeat(np.sin(angle), SUB, axis=1)
    rows = np.zeros((512, 512))
    first, second = np.meshgrid(np.arange(32), np.arange(16), indexing="ij")
    rows[(second * 32 + first).ravel(), (first * 16 + second).ravel()] = 1.0
    filt_rows = np.zeros((512, 512))
    first, second, part = np.meshgrid(
        np.arange(16), np.arange(16), np.arange(2), indexing="ij"
    )
    filt_rows[
        (part * 256 + second * 16 + first).ravel(), (first * 32 + second * 2 + part).ravel()
    ] = 1.0
    lanes = np.zeros((1024, 1024))
    outer, inner, chan = np.meshgrid(np.arange(8), np.arange(8), np.arange(16), indexing="ij")
    lanes[
        (outer * 128 + inner * 16 + chan).ravel(), (inner * 128 + outer * 16 + chan).ravel()
    ] = 1.0

    def half(array):
        return array.astype(np.float32).astype(ml_dtypes.bfloat16)

    return (
        half(np.stack([rows, rows.T, filt_rows])),
        half(lanes),
        half(long_rows),
        half(long_cols),
        np.stack([twist_cos, twist_sin]).astype(np.float32),
        half(np.stack([forth, back])),
    )


def dot(left, right):
    return jnp.dot(left, right, preferred_element_type=F32)


def arrive(ref, sem):
    pltpu.make_async_copy(ref, ref, sem).wait()


def kernel(
    query,
    key,
    value,
    filt,
    weight,
    moves,
    lanes_table,
    rows_table,
    cols_table,
    twist,
    short_table,
    out,
    query_v,
    key_v,
    value_v,
    filt_v,
    moves_v,
    lanes_v,
    rows_v,
    cols_v,
    twist_v,
    short_v,
    sorted_v,
    filt_sorted,
    prod_send,
    prod_recv,
    filt_send,
    filt_recv,
    field,
    total,
    conv_send,
    conv_recv,
    gated,
    weights,
    ring_send,
    ring_recv,
    local_sem,
    prod_ss,
    prod_rs,
    filt_ss,
    filt_rs,
    conv_ss,
    conv_rs,
    weight_ss,
    weight_rs,
    share_rs,
    gate_ss,
    gate_rs,
    ring_ss,
    ring_rs,
):
    chan = lax.axis_index("chan")
    me = lax.axis_index("seq")
    y_lo, z, core = chan // 16, (chan // 2) % 8, chan % 2
    y_hi, x = me // 4, me % 4

    def chan_of(low, depth, which):
        return (low * 8 + depth) * 2 + which

    sibling = {"chan": chan_of(y_lo, z, 1 - core), "seq": me}
    across = {"chan": chan_of(1 - y_lo, z, core), "seq": me}
    far = (1 - y_hi) * 4 + x
    z_up = (z + 1) % 8
    z_down = (z + 7) % 8

    local = [
        (key, key_v),
        (value, value_v),
        (moves, moves_v),
        (lanes_table, lanes_v),
        (filt, filt_v),
        (rows_table, rows_v),
        (twist, twist_v),
        (short_table, short_v),
        (cols_table, cols_v),
        (query, query_v),
    ]

    def local_start(*places):
        for at in places:
            pltpu.make_async_copy(local[at][0], local[at][1], local_sem.at[at]).start()

    def local_done(*places):
        for at in places:
            pltpu.make_async_copy(local[at][0], local[at][1], local_sem.at[at]).wait()

    local_start(0, 1, 2, 3, 4)

    barrier = pltpu.get_barrier_semaphore()

    def greet(step, carry):
        peer = (me + step) % SEQ
        pl.semaphore_signal(barrier, 1, device_id={"chan": chan, "seq": peer}, device_id_type=MESH)
        return carry

    lax.fori_loop(1, SEQ, greet, 0)
    for peer in (
        sibling,
        {"chan": chan_of(y_lo, z_up, core), "seq": me},
        {"chan": chan_of(y_lo, z_down, core), "seq": me},
        across,
        {"chan": chan_of(1 - y_lo, z, 1 - core), "seq": me},
        {"chan": chan_of(1 - y_lo, z, core), "seq": far},
        {"chan": chan_of(1 - y_lo, z, 1 - core), "seq": far},
    ):
        pl.semaphore_signal(barrier, 1, device_id=peer, device_id_type=MESH)


    def weight_block(low, depth, which):
        at = pl.multiple_of(chan_of(low, depth, which) * 256, 256)
        return weight.at[:, pl.ds(at, 256)]

    def send_weight_near(depth):
        pltpu.make_async_copy(
            weight_block(y_lo, depth, core), weights.at[depth, pl.ds(0, 256), :], weight_rs.at[depth]
        ).start()
        pltpu.make_async_remote_copy(
            weight_block(y_lo, depth, 1 - core),
            weights.at[depth, pl.ds(256, 256), :],
            weight_ss,
            weight_rs.at[depth],
            device_id=sibling,
            device_id_type=MESH,
        ).start()

    core_across = (core + x // 2) % 2
    row_across = pl.multiple_of((x % 2) * 128, 128)
    row_shared = pl.multiple_of(512 + x * 128, 128)

    def send_weight_across(step, seq_to):
        depth = (z + step) % 8
        at = pl.multiple_of(chan_of(1 - y_lo, depth, core_across) * 256, 256)
        pltpu.make_async_remote_copy(
            weight.at[pl.ds(row_across, 128), pl.ds(at, 256)],
            weights.at[depth, pl.ds(row_shared, 128), :],
            weight_ss,
            share_rs,
            device_id={"chan": chan_of(1 - y_lo, z, core_across), "seq": seq_to},
            device_id_type=MESH,
        ).start()

    def share_weight(step):
        depth = (z + step) % 8
        shared = weights.at[depth, pl.ds(row_shared, 128), :]
        for peer in (1, 3, 2):
            pltpu.make_async_remote_copy(
                shared,
                shared,
                weight_ss,
                weight_rs.at[depth],
                device_id={"chan": chan, "seq": y_hi * 4 + (x + peer) % 4},
                device_id_type=MESH,
            ).start()

    local_done(0, 1, 2)
    for half in range(2):
        rows = pl.ds(half * 512, 512)
        product = (key_v[rows, :].astype(F32) * value_v[rows, :].astype(F32)).astype(BF)
        moved = dot(moves_v[0], product).astype(BF)
        sorted_v[:, pl.ds(half * 32, 32), :] = moved.reshape(SHORT, 32, 256)
    local_done(3)
    for share in range(SHARES):
        block = jnp.concatenate(
            [
                jnp.concatenate(
                    [sorted_v[8 * group + b, :, pl.ds(share * 128, 128)] for b in range(8)], axis=1
                )
                for group in range(2)
            ],
            axis=0,
        )
        moved = dot(block, lanes_v[...]).astype(BF)
        for owner in range(SEQ):
            for group in range(2):
                prod_send[share, owner, :, pl.ds(group * 128, 128)] = moved[
                    group * 64 : (group + 1) * 64, owner * 128 : (owner + 1) * 128
                ]


    def spread(send, recv, ss, rs):
        def one(step, carry):
            peer = (me + step) % SEQ
            pltpu.make_async_remote_copy(
                send.at[peer],
                recv.at[me],
                ss,
                rs,
                device_id={"chan": chan, "seq": peer},
                device_id_type=MESH,
            ).start()
            return carry

        lax.fori_loop(1, SEQ, one, 0)
        pltpu.make_async_copy(send.at[me], recv.at[me], rs).start()

    pl.semaphore_wait(barrier, SEQ - 1 + 7)
    for share in range(SHARES):
        spread(prod_send.at[share], prod_recv.at[share], prod_ss.at[share], prod_rs.at[share])
    for step, seq_to in ((1, me), (7, far), (2, far), (6, me), (3, me), (5, far), (4, me), (0, far)):
        send_weight_across(step, seq_to)

    local_start(5, 6, 7)
    local_done(4)

    def send_filter(share, wave):
        block = jnp.concatenate(
            [
                jnp.concatenate(
                    [
                        filt_sorted[wave, at, 8 * group + b, :, pl.ds(share * 128, 128)]
                        for b in range(8)
                    ],
                    axis=1,
                )
                for at in range(2)
                for group in range(2)
            ],
            axis=0,
        )
        moved = dot(block, lanes_v[...]).astype(BF)
        for owner in range(SEQ):
            for at in range(2):
                for group in range(2):
                    first = (at * 2 + group) * WAVE_ROWS
                    filt_send[share, wave, owner, at, :, pl.ds(group * 128, 128)] = moved[
                        first : first + WAVE_ROWS, owner * 128 : (owner + 1) * 128
                    ]
        spread(
            filt_send.at[share, wave],
            filt_recv.at[share, wave],
            filt_ss.at[share, wave],
            filt_rs.at[share, wave],
        )

    def sort_filter(wave, carry):
        for at in range(2):
            block = filt_v[pl.ds((2 * wave + at) * 16, 16)].reshape(512, 256)
            moved = dot(moves_v[2], block).astype(BF)
            filt_sorted[wave, :, :, pl.ds(at * 16, 16), :] = moved.reshape(2, SHORT, 16, 256)
        send_filter(0, wave)
        return carry

    def rest_of_filter(wave, carry):
        send_filter(1, wave)
        return carry

    lax.fori_loop(0, WAVES, sort_filter, 0)
    lax.fori_loop(0, WAVES, rest_of_filter, 0)
    local_start(8, 9)


    local_done(5, 6, 7)

    def forward(at, carry):
        share, step = at // 4, at % 4

        @pl.when(step == 0)
        def _():
            arrive(prod_recv.at[share], prod_rs.at[share])

        rows = pl.ds(pl.multiple_of(step * 256, 256), 256)
        values = prod_recv[share].reshape(512, LANES)
        real = dot(rows_v[0, rows, :], values)
        imag = dot(rows_v[1, rows, :], values)
        tw_cos = twist_v[0, rows, :]
        tw_sin = twist_v[1, rows, :]
        both = jnp.concatenate(
            [
                (real * tw_cos + imag * tw_sin).astype(BF),
                (imag * tw_cos - real * tw_sin).astype(BF),
            ],
            axis=1,
        )
        field[share, rows, :] = dot(both, short_v[0])
        return carry

    lax.fori_loop(0, SHARES * 4, forward, 0)
    local_done(8)

    def inverse(share):
        total[...] = jnp.zeros_like(total)

        def backward(wave, carry):
            arrive(filt_recv.at[share, wave], filt_rs.at[share, wave])
            rows = pl.ds(pl.multiple_of(wave * 256, 256), 256)
            real = field[share, rows, pl.ds(0, LANES)]
            imag = field[share, rows, pl.ds(LANES, LANES)]
            filt_real = filt_recv[share, wave, :, 0].reshape(256, LANES).astype(F32)
            filt_imag = filt_recv[share, wave, :, 1].reshape(256, LANES).astype(F32)
            both = jnp.concatenate(
                [
                    (real * filt_real - imag * filt_imag).astype(BF),
                    (real * filt_imag + imag * filt_real).astype(BF),
                ],
                axis=1,
            )
            mixed = dot(both, short_v[1])
            real = mixed[:, :LANES]
            imag = mixed[:, LANES:]
            tw_cos = twist_v[0, rows, :]
            tw_sin = twist_v[1, rows, :]
            turned = jnp.concatenate(
                [
                    (real * tw_cos - imag * tw_sin).astype(BF),
                    (imag * tw_cos + real * tw_sin).astype(BF),
                ],
                axis=0,
            )
            table = jnp.concatenate([cols_v[0, :, rows], cols_v[1, :, rows]], axis=1)
            total[...] += dot(table, turned)
            return carry

        lax.fori_loop(0, WAVES, backward, 0)
        conv_send[share] = (total[...] * (1.0 / TOTAL)).astype(BF).reshape(SEQ, 64, LANES)
        spread(conv_send.at[share], conv_recv.at[share], conv_ss.at[share], conv_rs.at[share])

    def rows_of(piece):
        return pl.ds(pl.multiple_of(piece * PIECE, PIECE), PIECE)

    def part(piece, slot, share):
        return gated.at[rows_of(piece), pl.ds(slot * 256 + share * 128, 128)]

    def gate_copy(kind, piece, share, source, target, device):
        return pltpu.make_async_remote_copy(
            part(piece, source, share),
            part(piece, target, share),
            gate_ss.at[kind, share],
            gate_rs.at[kind, share, piece],
            device_id=device,
            device_id_type=MESH,
        )

    def piece_of(at):
        return (at % 2) * STREAMS + at // 2

    def gate(share):
        arrive(conv_recv.at[share], conv_rs.at[share])
        lanes = pl.ds(share * 128, 128)
        block = jnp.concatenate(
            [
                jnp.concatenate(
                    [conv_recv[share, owner, :, pl.ds(group * 128, 128)] for owner in range(SEQ)],
                    axis=1,
                )
                for group in range(2)
            ],
            axis=0,
        )
        moved = dot(block, lanes_v[...]).astype(BF)
        for group in range(2):
            for b in range(8):
                sorted_v[8 * group + b, :, lanes] = moved[
                    group * 64 : (group + 1) * 64, b * 128 : (b + 1) * 128
                ]
        for half in range(2):
            rows = pl.ds(half * 512, 512)
            block = sorted_v[:, pl.ds(half * 32, 32), lanes].reshape(512, 128)
            conv = dot(moves_v[1], block)
            gated[rows, lanes] = (query_v[rows, lanes].astype(F32) * conv).astype(BF)

        def send_gated(at, carry):
            piece = piece_of(at)
            gate_copy(0, piece, share, 0, 2, across).start()
            gate_copy(1, piece, share, 0, 1, sibling).start()
            return carry

        lax.fori_loop(0, 2 * STREAMS, send_gated, 0)

    def pass_on(piece, share):
        arrive(part(piece, 2, share), gate_rs.at[0, share, piece])
        gate_copy(2, piece, share, 2, 3, sibling).start()

    def gate_done(piece, share):
        arrive(part(piece, 1, share), gate_rs.at[1, share, piece])
        arrive(part(piece, 3, share), gate_rs.at[2, share, piece])

    local_done(9)
    inverse(0)
    inverse(1)

    def late_weights(depth, carry):
        send_weight_near(depth)
        return carry

    lax.fori_loop(0, 8, late_weights, 0)
    arrive(weights.at[0], share_rs)
    share_weight(1)
    share_weight(7)

    gate(0)

    def pass_first(at, carry):
        pass_on(piece_of(at), 0)
        return carry

    gate(1)
    lax.fori_loop(0, 2 * STREAMS, pass_first, 0)
    for step in (2, 6, 3, 5, 4, 0):
        share_weight(step)

    def wait_weight(step):
        depth = (z + step) % 8
        arrive(weights.at[depth, pl.ds(0, 896), :], weight_rs.at[depth])

    def term(piece, step):
        depth = (z + 7 - step) % 8 if piece // STREAMS == 0 else (z + 1 + step) % 8
        return dot(gated[rows_of(piece), :], weights[depth])

    def ring_copy(piece, step):
        depth = z_up if piece // STREAMS == 0 else z_down
        return pltpu.make_async_remote_copy(
            ring_send.at[piece, step],
            ring_recv.at[piece, step],
            ring_ss.at[piece],
            ring_rs.at[piece, step],
            device_id={"chan": chan_of(y_lo, depth, core), "seq": me},
            device_id_type=MESH,
        )

    wait_weight(1)
    wait_weight(7)
    for sub in range(STREAMS):
        for piece in (sub, sub + STREAMS):
            pass_on(piece, 1)
        for piece in (sub, sub + STREAMS):
            gate_done(piece, 0)
            gate_done(piece, 1)
            ring_send[piece, 0] = term(piece, 0).astype(BF)
            ring_copy(piece, 0).start()

    def ring_step(step, carry):
        @pl.when(step < 4)
        def _():
            wait_weight(1 + step)

        @pl.when(step < 3)
        def _():
            wait_weight(7 - step)

        for sub in range(STREAMS):
            for piece in (sub, sub + STREAMS):
                own = term(piece, step)
                ring_copy(piece, step - 1).wait_recv()
                ring_send[piece, step] = (own + ring_recv[piece, step - 1].astype(F32)).astype(BF)
                ring_copy(piece, step).start()
        return carry

    lax.fori_loop(1, 7, ring_step, 0)
    wait_weight(0)
    for sub in range(STREAMS):
        for piece in (sub, sub + STREAMS):
            own = term(piece, 7)
            ring_copy(piece, 6).wait_recv()
            out[rows_of(piece), :] = (own + ring_recv[piece, 6].astype(F32)).astype(BF)

    for share in range(SHARES):
        arrive(prod_send.at[share, pl.ds(0, SEQ - 1)], prod_ss.at[share])
        arrive(conv_send.at[share, pl.ds(0, SEQ - 1)], conv_ss.at[share])
        for wave in range(WAVES):
            arrive(filt_send.at[share, wave, pl.ds(0, SEQ - 1)], filt_ss.at[share, wave])
        for kind in range(3):
            arrive(gated.at[:, pl.ds(0, 128)], gate_ss.at[kind, share])
    arrive(weights.at[pl.ds(0, 6)], weight_ss)
    for piece in range(2 * STREAMS):
        arrive(ring_send.at[piece], ring_ss.at[piece])


def body(query_input, key_input, value_input, filter_spectrum, out_weight):
    moves, lanes_table, rows_table, cols_table, twist, short_table = make_tables()
    anywhere = pl.BlockSpec(memory_space=pl.ANY)
    dma = pltpu.SemaphoreType.DMA
    mixed = pl.pallas_call(
        kernel,
        out_shape=pltpu.VMEM((1024, 256), BF),
        in_specs=[anywhere] * 11,
        out_specs=pl.BlockSpec(memory_space=pltpu.VMEM),
        scratch_shapes=[
            pltpu.VMEM((1024, 256), BF),
            pltpu.VMEM((1024, 256), BF),
            pltpu.VMEM((1024, 256), BF),
            pltpu.VMEM((128, SHORT, 2, 256), BF),
            pltpu.VMEM((3, 512, 512), BF),
            pltpu.VMEM((1024, 1024), BF),
            pltpu.VMEM((2, ORDER, ORDER // 2), BF),
            pltpu.VMEM((2, ORDER // 2, ORDER), BF),
            pltpu.VMEM((2, ORDER, LANES), F32),
            pltpu.VMEM((2, 2 * LANES, 2 * LANES), BF),
            pltpu.VMEM((SHORT, 64, 256), BF),
            pltpu.VMEM((WAVES, 2, SHORT, WAVE_ROWS, 256), BF),
            pltpu.VMEM((SHARES, SEQ, 64, LANES), BF),
            pltpu.VMEM((SHARES, SEQ, 64, LANES), BF),
            pltpu.VMEM((SHARES, WAVES, SEQ, 2, WAVE_ROWS, LANES), BF),
            pltpu.VMEM((SHARES, WAVES, SEQ, 2, WAVE_ROWS, LANES), BF),
            pltpu.VMEM((SHARES, ORDER, 2 * LANES), F32),
            pltpu.VMEM((512, LANES), F32),
            pltpu.VMEM((SHARES, SEQ, 64, LANES), BF),
            pltpu.VMEM((SHARES, SEQ, 64, LANES), BF),
            pltpu.VMEM((1024, 1024), BF),
            pltpu.VMEM((8, 1024, 256), BF),
            pltpu.VMEM((2 * STREAMS, 7, PIECE, 256), BF),
            pltpu.VMEM((2 * STREAMS, 7, PIECE, 256), BF),
            dma((10,)),
            dma((SHARES,)),
            dma((SHARES,)),
            dma((SHARES, WAVES)),
            dma((SHARES, WAVES)),
            dma((SHARES,)),
            dma((SHARES,)),
            dma,
            dma((8,)),
            dma,
            dma((3, SHARES)),
            dma((3, SHARES, 2 * STREAMS)),
            dma((2 * STREAMS,)),
            dma((2 * STREAMS, 7)),
        ],
        compiler_params=pltpu.CompilerParams(
            collective_id=0, has_side_effects=True, vmem_limit_bytes=58 * 2**20
        ),
        name="hyena",
    )(
        query_input,
        key_input,
        value_input,
        filter_spectrum,
        out_weight,
        jnp.asarray(moves),
        jnp.asarray(lanes_table),
        jnp.asarray(rows_table),
        jnp.asarray(cols_table),
        jnp.asarray(twist),
        jnp.asarray(short_table),
    )
    return mixed.T


def solution(mesh):
    in_specs = (
        P("seq", "chan"),
        P("seq", "chan"),
        P("seq", "chan"),
        P("seq", None, None, "chan"),
        P("chan", None),
    )
    return jax.shard_map(
        body, mesh=mesh, in_specs=in_specs, out_specs=P("chan", "seq"), check_vma=False
    )
```

```python
import functools
import math

import jax
import jax.numpy as jnp
import ml_dtypes
import numpy as np
from jax import lax
from jax.experimental import pallas as pl
from jax.experimental.pallas import tpu as pltpu
from jax.sharding import PartitionSpec as P

BF = jnp.bfloat16
F32 = jnp.float32
ORDER = 1024
SHORT = 16
TOTAL = ORDER * SHORT
SEQ = 8
SHARES = 2
SUB = 16
LANES = SHORT * SUB
MESH = pl.DeviceIdType.MESH
WAVES = 4
WAVE_ROWS = ORDER // SEQ // WAVES
STREAMS = 4
PIECE = 512 // STREAMS


def make_tables():
    step = np.arange(ORDER)
    angle = 2.0 * math.pi / ORDER * (np.outer(step, step) % ORDER)
    order = step.reshape(SEQ, WAVES, WAVE_ROWS).transpose(1, 0, 2).ravel()
    long = np.stack([np.cos(angle), -np.sin(angle)])
    long_rows = long[:, order, : ORDER // 2]
    long_cols = long[:, : ORDER // 2, order]
    short = np.arange(SHORT)
    angle = 2.0 * math.pi / SHORT * (np.outer(short, short) % SHORT)
    eye = np.eye(SUB)
    short_cos = np.kron(np.cos(angle), eye)
    short_sin = np.kron(np.sin(angle), eye)
    forth = np.block([[short_cos, -short_sin], [short_sin, short_cos]])
    back = np.block([[short_cos, short_sin], [-short_sin, short_cos]])
    angle = 2.0 * math.pi / TOTAL * np.outer(step, short)[order]
    twist_cos = np.repeat(np.cos(angle), SUB, axis=1)
    twist_sin = np.repeat(np.sin(angle), SUB, axis=1)
    rows = np.zeros((512, 512))
    first, second = np.meshgrid(np.arange(32), np.arange(16), indexing="ij")
    rows[(second * 32 + first).ravel(), (first * 16 + second).ravel()] = 1.0
    filt_rows = np.zeros((512, 512))
    first, second, part = np.meshgrid(
        np.arange(16), np.arange(16), np.arange(2), indexing="ij"
    )
    filt_rows[
        (part * 256 + second * 16 + first).ravel(), (first * 32 + second * 2 + part).ravel()
    ] = 1.0
    lanes = np.zeros((1024, 1024))
    outer, inner, chan = np.meshgrid(np.arange(8), np.arange(8), np.arange(16), indexing="ij")
    lanes[
        (outer * 128 + inner * 16 + chan).ravel(), (inner * 128 + outer * 16 + chan).ravel()
    ] = 1.0

    def half(array):
        return array.astype(np.float32).astype(ml_dtypes.bfloat16)

    return (
        half(np.stack([rows, rows.T, filt_rows])),
        half(lanes),
        half(long_rows),
        half(long_cols),
        np.stack([twist_cos, twist_sin]).astype(np.float32),
        half(np.stack([forth, back])),
    )


def dot(left, right):
    return jnp.dot(left, right, preferred_element_type=F32)


def arrive(ref, sem):
    pltpu.make_async_copy(ref, ref, sem).wait()


def kernel(
    query,
    key,
    value,
    filt,
    weight,
    moves,
    lanes_table,
    rows_table,
    cols_table,
    twist,
    short_table,
    out,
    query_v,
    key_v,
    value_v,
    filt_v,
    moves_v,
    lanes_v,
    rows_v,
    cols_v,
    twist_v,
    short_v,
    sorted_v,
    filt_sorted,
    prod_send,
    prod_recv,
    filt_send,
    filt_recv,
    field,
    total,
    conv_send,
    conv_recv,
    gated,
    weights,
    ring_send,
    ring_recv,
    local_sem,
    prod_ss,
    prod_rs,
    filt_ss,
    filt_rs,
    conv_ss,
    conv_rs,
    weight_ss,
    weight_rs,
    share_rs,
    gate_ss,
    gate_rs,
    ring_ss,
    ring_rs,
):
    chan = lax.axis_index("chan")
    me = lax.axis_index("seq")
    y_lo, z, core = chan // 16, (chan // 2) % 8, chan % 2
    y_hi, x = me // 4, me % 4

    def chan_of(low, depth, which):
        return (low * 8 + depth) * 2 + which

    sibling = {"chan": chan_of(y_lo, z, 1 - core), "seq": me}
    across = {"chan": chan_of(1 - y_lo, z, core), "seq": me}
    far = (1 - y_hi) * 4 + x
    z_up = (z + 1) % 8
    z_down = (z + 7) % 8

    local = [
        (key, key_v),
        (value, value_v),
        (moves, moves_v),
        (lanes_table, lanes_v),
        (filt, filt_v),
        (rows_table, rows_v),
        (twist, twist_v),
        (short_table, short_v),
        (cols_table, cols_v),
        (query, query_v),
    ]

    def local_start(*places):
        for at in places:
            pltpu.make_async_copy(local[at][0], local[at][1], local_sem.at[at]).start()

    def local_done(*places):
        for at in places:
            pltpu.make_async_copy(local[at][0], local[at][1], local_sem.at[at]).wait()

    local_start(0, 1, 2, 3, 4)

    barrier = pltpu.get_barrier_semaphore()

    def greet(step, carry):
        peer = (me + step) % SEQ
        pl.semaphore_signal(barrier, 1, device_id={"chan": chan, "seq": peer}, device_id_type=MESH)
        return carry

    lax.fori_loop(1, SEQ, greet, 0)
    for peer in (
        sibling,
        {"chan": chan_of(y_lo, z_up, core), "seq": me},
        {"chan": chan_of(y_lo, z_down, core), "seq": me},
        across,
        {"chan": chan_of(1 - y_lo, z, 1 - core), "seq": me},
        {"chan": chan_of(1 - y_lo, z, core), "seq": far},
        {"chan": chan_of(1 - y_lo, z, 1 - core), "seq": far},
    ):
        pl.semaphore_signal(barrier, 1, device_id=peer, device_id_type=MESH)


    def weight_block(low, depth, which):
        at = pl.multiple_of(chan_of(low, depth, which) * 256, 256)
        return weight.at[:, pl.ds(at, 256)]

    def send_weight_near(depth):
        pltpu.make_async_copy(
            weight_block(y_lo, depth, core), weights.at[depth, pl.ds(0, 256), :], weight_rs.at[depth]
        ).start()
        pltpu.make_async_remote_copy(
            weight_block(y_lo, depth, 1 - core),
            weights.at[depth, pl.ds(256, 256), :],
            weight_ss,
            weight_rs.at[depth],
            device_id=sibling,
            device_id_type=MESH,
        ).start()

    core_across = (core + x // 2) % 2
    row_across = pl.multiple_of((x % 2) * 128, 128)
    row_shared = pl.multiple_of(512 + x * 128, 128)

    def send_weight_across(step, seq_to, late):
        depth = (z + step) % 8
        at = pl.multiple_of(chan_of(1 - y_lo, depth, core_across) * 256, 256)
        pltpu.make_async_remote_copy(
            weight.at[pl.ds(row_across, 128), pl.ds(at, 256)],
            weights.at[depth, pl.ds(row_shared, 128), :],
            weight_ss,
            share_rs.at[late],
            device_id={"chan": chan_of(1 - y_lo, z, core_across), "seq": seq_to},
            device_id_type=MESH,
        ).start()

    def share_weight(step):
        depth = (z + step) % 8
        shared = weights.at[depth, pl.ds(row_shared, 128), :]
        for peer in (1, 3, 2):
            pltpu.make_async_remote_copy(
                shared,
                shared,
                weight_ss,
                weight_rs.at[depth],
                device_id={"chan": chan, "seq": y_hi * 4 + (x + peer) % 4},
                device_id_type=MESH,
            ).start()

    local_done(0, 1, 2)
    for half in range(2):
        rows = pl.ds(half * 512, 512)
        product = (key_v[rows, :].astype(F32) * value_v[rows, :].astype(F32)).astype(BF)
        moved = dot(moves_v[0], product).astype(BF)
        sorted_v[:, pl.ds(half * 32, 32), :] = moved.reshape(SHORT, 32, 256)
    local_done(3)
    for share in range(SHARES):
        block = jnp.concatenate(
            [
                jnp.concatenate(
                    [sorted_v[8 * group + b, :, pl.ds(share * 128, 128)] for b in range(8)], axis=1
                )
                for group in range(2)
            ],
            axis=0,
        )
        moved = dot(block, lanes_v[...]).astype(BF)
        for owner in range(SEQ):
            for group in range(2):
                prod_send[share, owner, :, pl.ds(group * 128, 128)] = moved[
                    group * 64 : (group + 1) * 64, owner * 128 : (owner + 1) * 128
                ]


    def spread(send, recv, ss, rs):
        def one(step, carry):
            peer = (me + step) % SEQ
            pltpu.make_async_remote_copy(
                send.at[peer],
                recv.at[me],
                ss,
                rs,
                device_id={"chan": chan, "seq": peer},
                device_id_type=MESH,
            ).start()
            return carry

        lax.fori_loop(1, SEQ, one, 0)
        pltpu.make_async_copy(send.at[me], recv.at[me], rs).start()

    pl.semaphore_wait(barrier, SEQ - 1 + 7)
    for share in range(SHARES):
        spread(prod_send.at[share], prod_recv.at[share], prod_ss.at[share], prod_rs.at[share])
    for step, seq_to in ((1, me), (7, far), (2, far), (6, me)):
        send_weight_across(step, seq_to, 0)

    local_start(5, 6, 7)
    local_done(4)

    def send_filter(share, wave):
        block = jnp.concatenate(
            [
                jnp.concatenate(
                    [
                        filt_sorted[wave, at, 8 * group + b, :, pl.ds(share * 128, 128)]
                        for b in range(8)
                    ],
                    axis=1,
                )
                for at in range(2)
                for group in range(2)
            ],
            axis=0,
        )
        moved = dot(block, lanes_v[...]).astype(BF)
        for owner in range(SEQ):
            for at in range(2):
                for group in range(2):
                    first = (at * 2 + group) * WAVE_ROWS
                    filt_send[share, wave, owner, at, :, pl.ds(group * 128, 128)] = moved[
                        first : first + WAVE_ROWS, owner * 128 : (owner + 1) * 128
                    ]
        spread(
            filt_send.at[share, wave],
            filt_recv.at[share, wave],
            filt_ss.at[share, wave],
            filt_rs.at[share, wave],
        )

    def sort_filter(wave, carry):
        for at in range(2):
            block = filt_v[pl.ds((2 * wave + at) * 16, 16)].reshape(512, 256)
            moved = dot(moves_v[2], block).astype(BF)
            filt_sorted[wave, :, :, pl.ds(at * 16, 16), :] = moved.reshape(2, SHORT, 16, 256)
        send_filter(0, wave)
        return carry

    def rest_of_filter(wave, carry):
        send_filter(1, wave)
        return carry

    lax.fori_loop(0, WAVES, sort_filter, 0)
    lax.fori_loop(0, WAVES, rest_of_filter, 0)
    local_start(8, 9)


    local_done(5, 6, 7)

    def forward(at, carry):
        share, step = at // 4, at % 4

        @pl.when(step == 0)
        def _():
            arrive(prod_recv.at[share], prod_rs.at[share])

        rows = pl.ds(pl.multiple_of(step * 256, 256), 256)
        values = prod_recv[share].reshape(512, LANES)
        real = dot(rows_v[0, rows, :], values)
        imag = dot(rows_v[1, rows, :], values)
        tw_cos = twist_v[0, rows, :]
        tw_sin = twist_v[1, rows, :]
        both = jnp.concatenate(
            [
                (real * tw_cos + imag * tw_sin).astype(BF),
                (imag * tw_cos - real * tw_sin).astype(BF),
            ],
            axis=1,
        )
        field[share, rows, :] = dot(both, short_v[0])
        return carry

    lax.fori_loop(0, SHARES * 4, forward, 0)
    local_done(8)

    def inverse(share):
        total[...] = jnp.zeros_like(total)

        def backward(wave, carry):
            arrive(filt_recv.at[share, wave], filt_rs.at[share, wave])
            rows = pl.ds(pl.multiple_of(wave * 256, 256), 256)
            real = field[share, rows, pl.ds(0, LANES)]
            imag = field[share, rows, pl.ds(LANES, LANES)]
            filt_real = filt_recv[share, wave, :, 0].reshape(256, LANES).astype(F32)
            filt_imag = filt_recv[share, wave, :, 1].reshape(256, LANES).astype(F32)
            both = jnp.concatenate(
                [
                    (real * filt_real - imag * filt_imag).astype(BF),
                    (real * filt_imag + imag * filt_real).astype(BF),
                ],
                axis=1,
            )
            mixed = dot(both, short_v[1])
            real = mixed[:, :LANES]
            imag = mixed[:, LANES:]
            tw_cos = twist_v[0, rows, :]
            tw_sin = twist_v[1, rows, :]
            turned = jnp.concatenate(
                [
                    (real * tw_cos - imag * tw_sin).astype(BF),
                    (imag * tw_cos + real * tw_sin).astype(BF),
                ],
                axis=0,
            )
            table = jnp.concatenate([cols_v[0, :, rows], cols_v[1, :, rows]], axis=1)
            total[...] += dot(table, turned)
            return carry

        lax.fori_loop(0, WAVES, backward, 0)
        conv_send[share] = (total[...] * (1.0 / TOTAL)).astype(BF).reshape(SEQ, 64, LANES)
        spread(conv_send.at[share], conv_recv.at[share], conv_ss.at[share], conv_rs.at[share])

    def rows_of(piece):
        return pl.ds(pl.multiple_of(piece * PIECE, PIECE), PIECE)

    def part(piece, slot, share):
        return gated.at[slot * SHARES + share, rows_of(piece), :]

    def gate_copy(kind, piece, share, source, target, device):
        return pltpu.make_async_remote_copy(
            part(piece, source, share),
            part(piece, target, share),
            gate_ss.at[kind, share],
            gate_rs.at[kind, share, piece],
            device_id=device,
            device_id_type=MESH,
        )

    def piece_of(at):
        return (at % 2) * STREAMS + at // 2

    def gate(share):
        arrive(conv_recv.at[share], conv_rs.at[share])
        lanes = pl.ds(share * 128, 128)
        block = jnp.concatenate(
            [
                jnp.concatenate(
                    [conv_recv[share, owner, :, pl.ds(group * 128, 128)] for owner in range(SEQ)],
                    axis=1,
                )
                for group in range(2)
            ],
            axis=0,
        )
        moved = dot(block, lanes_v[...]).astype(BF)
        for group in range(2):
            for b in range(8):
                sorted_v[8 * group + b, :, lanes] = moved[
                    group * 64 : (group + 1) * 64, b * 128 : (b + 1) * 128
                ]
        for half in range(2):
            rows = pl.ds(half * 512, 512)
            block = sorted_v[:, pl.ds(half * 32, 32), lanes].reshape(512, 128)
            conv = dot(moves_v[1], block)
            gated[share, rows, :] = (query_v[rows, lanes].astype(F32) * conv).astype(BF)

        def send_gated(at, carry):
            piece = piece_of(at)
            gate_copy(0, piece, share, 0, 2, across).start()
            gate_copy(1, piece, share, 0, 1, sibling).start()
            return carry

        lax.fori_loop(0, 2 * STREAMS, send_gated, 0)

    def pass_on(piece, share):
        arrive(part(piece, 2, share), gate_rs.at[0, share, piece])
        gate_copy(2, piece, share, 2, 3, sibling).start()

    def gate_done(piece, share):
        arrive(part(piece, 1, share), gate_rs.at[1, share, piece])
        arrive(part(piece, 3, share), gate_rs.at[2, share, piece])

    local_done(9)
    inverse(0)
    inverse(1)
    gate(0)

    def late_weights(depth, carry):
        send_weight_near(depth)
        return carry

    lax.fori_loop(0, 8, late_weights, 0)
    arrive(weights.at[0, pl.ds(0, 512), :], share_rs.at[0])
    share_weight(1)
    share_weight(7)

    def pass_first(at, carry):
        pass_on(piece_of(at), 0)
        return carry

    gate(1)
    lax.fori_loop(0, 2 * STREAMS, pass_first, 0)
    for step in (3, 5, 4, 0):
        send_weight_across(step, far, 1)
    share_weight(2)
    share_weight(6)

    def wait_weight(step):
        depth = (z + step) % 8
        arrive(weights.at[depth, pl.ds(0, 896), :], weight_rs.at[depth])

    def term(piece, step):
        depth = (z + 7 - step) % 8 if piece // STREAMS == 0 else (z + 1 + step) % 8
        rows = rows_of(piece)
        values = jnp.concatenate([gated[at, rows, :] for at in range(4 * SHARES)], axis=1)
        return dot(values, weights[depth])

    def ring_copy(piece, step):
        depth = z_up if piece // STREAMS == 0 else z_down
        return pltpu.make_async_remote_copy(
            ring_send.at[piece, step],
            ring_recv.at[piece, step],
            ring_ss.at[piece],
            ring_rs.at[piece, step],
            device_id={"chan": chan_of(y_lo, depth, core), "seq": me},
            device_id_type=MESH,
        )

    wait_weight(1)
    wait_weight(7)
    for sub in range(STREAMS):
        for piece in (sub, sub + STREAMS):
            pass_on(piece, 1)
        for piece in (sub, sub + STREAMS):
            gate_done(piece, 0)
            gate_done(piece, 1)
            ring_send[piece, 0] = term(piece, 0).astype(BF)
            ring_copy(piece, 0).start()

    arrive(weights.at[0, pl.ds(0, 512), :], share_rs.at[1])
    for step in (3, 5, 4, 0):
        share_weight(step)

    def ring_step(step, carry):
        @pl.when(step < 4)
        def _():
            wait_weight(1 + step)

        @pl.when(step < 3)
        def _():
            wait_weight(7 - step)

        for sub in range(STREAMS):
            for piece in (sub, sub + STREAMS):
                own = term(piece, step)
                ring_copy(piece, step - 1).wait_recv()
                ring_send[piece, step] = (own + ring_recv[piece, step - 1].astype(F32)).astype(BF)
                ring_copy(piece, step).start()
        return carry

    lax.fori_loop(1, 7, ring_step, 0)
    wait_weight(0)
    for sub in range(STREAMS):
        for piece in (sub, sub + STREAMS):
            own = term(piece, 7)
            ring_copy(piece, 6).wait_recv()
            out[rows_of(piece), :] = (own + ring_recv[piece, 6].astype(F32)).astype(BF)

    for share in range(SHARES):
        arrive(prod_send.at[share, pl.ds(0, SEQ - 1)], prod_ss.at[share])
        arrive(conv_send.at[share, pl.ds(0, SEQ - 1)], conv_ss.at[share])
        for wave in range(WAVES):
            arrive(filt_send.at[share, wave, pl.ds(0, SEQ - 1)], filt_ss.at[share, wave])
        for kind in range(3):
            arrive(gated.at[0], gate_ss.at[kind, share])
    arrive(weights.at[pl.ds(0, 6)], weight_ss)
    for piece in range(2 * STREAMS):
        arrive(ring_send.at[piece], ring_ss.at[piece])


def body(query_input, key_input, value_input, filter_spectrum, out_weight):
    moves, lanes_table, rows_table, cols_table, twist, short_table = make_tables()
    anywhere = pl.BlockSpec(memory_space=pl.ANY)
    dma = pltpu.SemaphoreType.DMA
    mixed = pl.pallas_call(
        kernel,
        out_shape=pltpu.VMEM((1024, 256), BF),
        in_specs=[anywhere] * 11,
        out_specs=pl.BlockSpec(memory_space=pltpu.VMEM),
        scratch_shapes=[
            pltpu.VMEM((1024, 256), BF),
            pltpu.VMEM((1024, 256), BF),
            pltpu.VMEM((1024, 256), BF),
            pltpu.VMEM((128, SHORT, 2, 256), BF),
            pltpu.VMEM((3, 512, 512), BF),
            pltpu.VMEM((1024, 1024), BF),
            pltpu.VMEM((2, ORDER, ORDER // 2), BF),
            pltpu.VMEM((2, ORDER // 2, ORDER), BF),
            pltpu.VMEM((2, ORDER, LANES), F32),
            pltpu.VMEM((2, 2 * LANES, 2 * LANES), BF),
            pltpu.VMEM((SHORT, 64, 256), BF),
            pltpu.VMEM((WAVES, 2, SHORT, WAVE_ROWS, 256), BF),
            pltpu.VMEM((SHARES, SEQ, 64, LANES), BF),
            pltpu.VMEM((SHARES, SEQ, 64, LANES), BF),
            pltpu.VMEM((SHARES, WAVES, SEQ, 2, WAVE_ROWS, LANES), BF),
            pltpu.VMEM((SHARES, WAVES, SEQ, 2, WAVE_ROWS, LANES), BF),
            pltpu.VMEM((SHARES, ORDER, 2 * LANES), F32),
            pltpu.VMEM((512, LANES), F32),
            pltpu.VMEM((SHARES, SEQ, 64, LANES), BF),
            pltpu.VMEM((SHARES, SEQ, 64, LANES), BF),
            pltpu.VMEM((4 * SHARES, 1024, 128), BF),
            pltpu.VMEM((8, 1024, 256), BF),
            pltpu.VMEM((2 * STREAMS, 7, PIECE, 256), BF),
            pltpu.VMEM((2 * STREAMS, 7, PIECE, 256), BF),
            dma((10,)),
            dma((SHARES,)),
            dma((SHARES,)),
            dma((SHARES, WAVES)),
            dma((SHARES, WAVES)),
            dma((SHARES,)),
            dma((SHARES,)),
            dma,
            dma((8,)),
            dma((2,)),
            dma((3, SHARES)),
            dma((3, SHARES, 2 * STREAMS)),
            dma((2 * STREAMS,)),
            dma((2 * STREAMS, 7)),
        ],
        compiler_params=pltpu.CompilerParams(
            collective_id=0, has_side_effects=True, vmem_limit_bytes=58 * 2**20
        ),
        name="hyena",
    )(
        query_input,
        key_input,
        value_input,
        filter_spectrum,
        out_weight,
        jnp.asarray(moves),
        jnp.asarray(lanes_table),
        jnp.asarray(rows_table),
        jnp.asarray(cols_table),
        jnp.asarray(twist),
        jnp.asarray(short_table),
    )
    return mixed.T


def solution(mesh):
    in_specs = (
        P("seq", "chan"),
        P("seq", "chan"),
        P("seq", "chan"),
        P("seq", None, None, "chan"),
        P("chan", None),
    )
    return jax.shard_map(
        body, mesh=mesh, in_specs=in_specs, out_specs=P("chan", "seq"), check_vma=False
    )
```

```python
import functools
import math

import jax
import jax.numpy as jnp
import ml_dtypes
import numpy as np
from jax import lax
from jax.experimental import pallas as pl
from jax.experimental.pallas import tpu as pltpu
from jax.sharding import PartitionSpec as P

BF = jnp.bfloat16
F32 = jnp.float32
ORDER = 1024
SHORT = 16
TOTAL = ORDER * SHORT
SEQ = 8
SHARES = 2
SUB = 16
LANES = SHORT * SUB
MESH = pl.DeviceIdType.MESH
WAVES = 4
WAVE_ROWS = ORDER // SEQ // WAVES
STREAMS = 4
PIECE = 512 // STREAMS


def make_tables():
    step = np.arange(ORDER)
    angle = 2.0 * math.pi / ORDER * (np.outer(step, step) % ORDER)
    order = step.reshape(SEQ, WAVES, WAVE_ROWS).transpose(1, 0, 2).ravel()
    long = np.stack([np.cos(angle), -np.sin(angle)])
    long_rows = long[:, order, : ORDER // 2]
    long_cols = long[:, : ORDER // 2, order]
    short = np.arange(SHORT)
    angle = 2.0 * math.pi / SHORT * (np.outer(short, short) % SHORT)
    eye = np.eye(SUB)
    short_cos = np.kron(np.cos(angle), eye)
    short_sin = np.kron(np.sin(angle), eye)
    forth = np.block([[short_cos, -short_sin], [short_sin, short_cos]])
    back = np.block([[short_cos, short_sin], [-short_sin, short_cos]])
    angle = 2.0 * math.pi / TOTAL * np.outer(step, short)[order]
    twist_cos = np.repeat(np.cos(angle), SUB, axis=1)
    twist_sin = np.repeat(np.sin(angle), SUB, axis=1)
    rows = np.zeros((512, 512))
    first, second = np.meshgrid(np.arange(32), np.arange(16), indexing="ij")
    rows[(second * 32 + first).ravel(), (first * 16 + second).ravel()] = 1.0
    filt_rows = np.zeros((512, 512))
    first, second, part = np.meshgrid(
        np.arange(16), np.arange(16), np.arange(2), indexing="ij"
    )
    filt_rows[
        (part * 256 + second * 16 + first).ravel(), (first * 32 + second * 2 + part).ravel()
    ] = 1.0
    lanes = np.zeros((1024, 1024))
    outer, inner, chan = np.meshgrid(np.arange(8), np.arange(8), np.arange(16), indexing="ij")
    lanes[
        (outer * 128 + inner * 16 + chan).ravel(), (inner * 128 + outer * 16 + chan).ravel()
    ] = 1.0

    def half(array):
        return array.astype(np.float32).astype(ml_dtypes.bfloat16)

    return (
        half(np.stack([rows, rows.T, filt_rows])),
        half(lanes),
        half(long_rows),
        half(long_cols),
        np.stack([twist_cos, twist_sin]).astype(np.float32),
        half(np.stack([forth, back])),
    )


def dot(left, right):
    return jnp.dot(left, right, preferred_element_type=F32)


def arrive(ref, sem):
    pltpu.make_async_copy(ref, ref, sem).wait()


def kernel(
    query,
    key,
    value,
    filt,
    weight,
    moves,
    lanes_table,
    rows_table,
    cols_table,
    twist,
    short_table,
    out,
    query_v,
    key_v,
    value_v,
    filt_v,
    moves_v,
    lanes_v,
    rows_v,
    cols_v,
    twist_v,
    short_v,
    sorted_v,
    filt_sorted,
    prod_send,
    prod_recv,
    filt_send,
    filt_recv,
    field,
    total,
    conv_send,
    conv_recv,
    gated,
    weights,
    ring_send,
    ring_recv,
    local_sem,
    prod_ss,
    prod_rs,
    filt_ss,
    filt_rs,
    conv_ss,
    conv_rs,
    weight_ss,
    weight_rs,
    share_rs,
    gate_ss,
    gate_rs,
    ring_ss,
    ring_rs,
):
    chan = lax.axis_index("chan")
    me = lax.axis_index("seq")
    y_lo, z, core = chan // 16, (chan // 2) % 8, chan % 2
    y_hi, x = me // 4, me % 4

    def chan_of(low, depth, which):
        return (low * 8 + depth) * 2 + which

    sibling = {"chan": chan_of(y_lo, z, 1 - core), "seq": me}
    across = {"chan": chan_of(1 - y_lo, z, core), "seq": me}
    far = (1 - y_hi) * 4 + x
    z_up = (z + 1) % 8
    z_down = (z + 7) % 8

    local = [
        (key, key_v),
        (value, value_v),
        (moves, moves_v),
        (lanes_table, lanes_v),
        (filt, filt_v),
        (rows_table, rows_v),
        (twist, twist_v),
        (short_table, short_v),
        (cols_table, cols_v),
        (query, query_v),
    ]

    def local_start(*places):
        for at in places:
            pltpu.make_async_copy(local[at][0], local[at][1], local_sem.at[at]).start()

    def local_done(*places):
        for at in places:
            pltpu.make_async_copy(local[at][0], local[at][1], local_sem.at[at]).wait()

    local_start(0, 1, 2, 3, 4)

    barrier = pltpu.get_barrier_semaphore()

    def greet(step, carry):
        peer = (me + step) % SEQ
        pl.semaphore_signal(barrier, 1, device_id={"chan": chan, "seq": peer}, device_id_type=MESH)
        return carry

    lax.fori_loop(1, SEQ, greet, 0)
    for peer in (
        sibling,
        {"chan": chan_of(y_lo, z_up, core), "seq": me},
        {"chan": chan_of(y_lo, z_down, core), "seq": me},
        across,
        {"chan": chan_of(1 - y_lo, z, 1 - core), "seq": me},
        {"chan": chan_of(1 - y_lo, z, core), "seq": far},
        {"chan": chan_of(1 - y_lo, z, 1 - core), "seq": far},
    ):
        pl.semaphore_signal(barrier, 1, device_id=peer, device_id_type=MESH)


    def weight_block(low, depth, which):
        at = pl.multiple_of(chan_of(low, depth, which) * 256, 256)
        return weight.at[:, pl.ds(at, 256)]

    def send_weight_near(depth):
        pltpu.make_async_copy(
            weight_block(y_lo, depth, core), weights.at[depth, pl.ds(0, 256), :], weight_rs.at[depth]
        ).start()
        pltpu.make_async_remote_copy(
            weight_block(y_lo, depth, 1 - core),
            weights.at[depth, pl.ds(256, 256), :],
            weight_ss,
            weight_rs.at[depth],
            device_id=sibling,
            device_id_type=MESH,
        ).start()

    core_across = (core + x // 2) % 2
    row_across = pl.multiple_of((x % 2) * 128, 128)
    row_shared = pl.multiple_of(512 + x * 128, 128)

    def send_weight_across(step, seq_to, late):
        depth = (z + step) % 8
        at = pl.multiple_of(chan_of(1 - y_lo, depth, core_across) * 256, 256)
        pltpu.make_async_remote_copy(
            weight.at[pl.ds(row_across, 128), pl.ds(at, 256)],
            weights.at[depth, pl.ds(row_shared, 128), :],
            weight_ss,
            share_rs.at[late],
            device_id={"chan": chan_of(1 - y_lo, z, core_across), "seq": seq_to},
            device_id_type=MESH,
        ).start()

    def share_weight(step):
        depth = (z + step) % 8
        shared = weights.at[depth, pl.ds(row_shared, 128), :]
        for peer in (1, 3, 2):
            pltpu.make_async_remote_copy(
                shared,
                shared,
                weight_ss,
                weight_rs.at[depth],
                device_id={"chan": chan, "seq": y_hi * 4 + (x + peer) % 4},
                device_id_type=MESH,
            ).start()

    local_done(0, 1, 2)
    for half in range(2):
        rows = pl.ds(half * 512, 512)
        product = (key_v[rows, :].astype(F32) * value_v[rows, :].astype(F32)).astype(BF)
        moved = dot(moves_v[0], product).astype(BF)
        sorted_v[:, pl.ds(half * 32, 32), :] = moved.reshape(SHORT, 32, 256)
    local_done(3)
    for share in range(SHARES):
        block = jnp.concatenate(
            [
                jnp.concatenate(
                    [sorted_v[8 * group + b, :, pl.ds(share * 128, 128)] for b in range(8)], axis=1
                )
                for group in range(2)
            ],
            axis=0,
        )
        moved = dot(block, lanes_v[...]).astype(BF)
        for owner in range(SEQ):
            for group in range(2):
                prod_send[share, owner, :, pl.ds(group * 128, 128)] = moved[
                    group * 64 : (group + 1) * 64, owner * 128 : (owner + 1) * 128
                ]


    def spread(send, recv, ss, rs):
        def one(step, carry):
            peer = (me + step) % SEQ
            pltpu.make_async_remote_copy(
                send.at[peer],
                recv.at[me],
                ss,
                rs,
                device_id={"chan": chan, "seq": peer},
                device_id_type=MESH,
            ).start()
            return carry

        lax.fori_loop(1, SEQ, one, 0)
        pltpu.make_async_copy(send.at[me], recv.at[me], rs).start()

    pl.semaphore_wait(barrier, SEQ - 1 + 7)
    for share in range(SHARES):
        spread(prod_send.at[share], prod_recv.at[share], prod_ss.at[share], prod_rs.at[share])
    for step, seq_to in ((1, me), (7, far)):
        send_weight_across(step, seq_to, 0)

    local_start(5, 6, 7)
    local_done(4)

    def send_filter(share, wave):
        block = jnp.concatenate(
            [
                jnp.concatenate(
                    [
                        filt_sorted[wave, at, 8 * group + b, :, pl.ds(share * 128, 128)]
                        for b in range(8)
                    ],
                    axis=1,
                )
                for at in range(2)
                for group in range(2)
            ],
            axis=0,
        )
        moved = dot(block, lanes_v[...]).astype(BF)
        for owner in range(SEQ):
            for at in range(2):
                for group in range(2):
                    first = (at * 2 + group) * WAVE_ROWS
                    filt_send[share, wave, owner, at, :, pl.ds(group * 128, 128)] = moved[
                        first : first + WAVE_ROWS, owner * 128 : (owner + 1) * 128
                    ]
        spread(
            filt_send.at[share, wave],
            filt_recv.at[share, wave],
            filt_ss.at[share, wave],
            filt_rs.at[share, wave],
        )

    def sort_filter(wave, carry):
        for at in range(2):
            block = filt_v[pl.ds((2 * wave + at) * 16, 16)].reshape(512, 256)
            moved = dot(moves_v[2], block).astype(BF)
            filt_sorted[wave, :, :, pl.ds(at * 16, 16), :] = moved.reshape(2, SHORT, 16, 256)
        send_filter(0, wave)
        return carry

    def rest_of_filter(wave, carry):
        send_filter(1, wave)
        return carry

    lax.fori_loop(0, WAVES, sort_filter, 0)
    lax.fori_loop(0, WAVES, rest_of_filter, 0)
    local_start(8, 9)


    local_done(5, 6, 7)

    def forward(at, carry):
        share, step = at // 4, at % 4

        @pl.when(step == 0)
        def _():
            arrive(prod_recv.at[share], prod_rs.at[share])

        rows = pl.ds(pl.multiple_of(step * 256, 256), 256)
        values = prod_recv[share].reshape(512, LANES)
        real = dot(rows_v[0, rows, :], values)
        imag = dot(rows_v[1, rows, :], values)
        tw_cos = twist_v[0, rows, :]
        tw_sin = twist_v[1, rows, :]
        both = jnp.concatenate(
            [
                (real * tw_cos + imag * tw_sin).astype(BF),
                (imag * tw_cos - real * tw_sin).astype(BF),
            ],
            axis=1,
        )
        field[share, rows, :] = dot(both, short_v[0])
        return carry

    lax.fori_loop(0, SHARES * 4, forward, 0)
    local_done(8)

    def inverse(share):
        total[...] = jnp.zeros_like(total)

        def backward(wave, carry):
            arrive(filt_recv.at[share, wave], filt_rs.at[share, wave])
            rows = pl.ds(pl.multiple_of(wave * 256, 256), 256)
            real = field[share, rows, pl.ds(0, LANES)]
            imag = field[share, rows, pl.ds(LANES, LANES)]
            filt_real = filt_recv[share, wave, :, 0].reshape(256, LANES).astype(F32)
            filt_imag = filt_recv[share, wave, :, 1].reshape(256, LANES).astype(F32)
            both = jnp.concatenate(
                [
                    (real * filt_real - imag * filt_imag).astype(BF),
                    (real * filt_imag + imag * filt_real).astype(BF),
                ],
                axis=1,
            )
            mixed = dot(both, short_v[1])
            real = mixed[:, :LANES]
            imag = mixed[:, LANES:]
            tw_cos = twist_v[0, rows, :]
            tw_sin = twist_v[1, rows, :]
            turned = jnp.concatenate(
                [
                    (real * tw_cos - imag * tw_sin).astype(BF),
                    (imag * tw_cos + real * tw_sin).astype(BF),
                ],
                axis=0,
            )
            table = jnp.concatenate([cols_v[0, :, rows], cols_v[1, :, rows]], axis=1)
            total[...] += dot(table, turned)
            return carry

        lax.fori_loop(0, WAVES, backward, 0)
        conv_send[share] = (total[...] * (1.0 / TOTAL)).astype(BF).reshape(SEQ, 64, LANES)
        spread(conv_send.at[share], conv_recv.at[share], conv_ss.at[share], conv_rs.at[share])

    def rows_of(piece):
        return pl.ds(pl.multiple_of(piece * PIECE, PIECE), PIECE)

    def part(piece, slot, share):
        return gated.at[slot * SHARES + share, rows_of(piece), :]

    def gate_copy(kind, piece, share, source, target, device):
        return pltpu.make_async_remote_copy(
            part(piece, source, share),
            part(piece, target, share),
            gate_ss.at[kind, share],
            gate_rs.at[kind, share, piece],
            device_id=device,
            device_id_type=MESH,
        )

    def piece_of(at):
        return (at % 2) * STREAMS + at // 2

    def gate(share):
        arrive(conv_recv.at[share], conv_rs.at[share])
        lanes = pl.ds(share * 128, 128)
        block = jnp.concatenate(
            [
                jnp.concatenate(
                    [conv_recv[share, owner, :, pl.ds(group * 128, 128)] for owner in range(SEQ)],
                    axis=1,
                )
                for group in range(2)
            ],
            axis=0,
        )
        moved = dot(block, lanes_v[...]).astype(BF)
        for group in range(2):
            for b in range(8):
                sorted_v[8 * group + b, :, lanes] = moved[
                    group * 64 : (group + 1) * 64, b * 128 : (b + 1) * 128
                ]
        for half in range(2):
            rows = pl.ds(half * 512, 512)
            block = sorted_v[:, pl.ds(half * 32, 32), lanes].reshape(512, 128)
            conv = dot(moves_v[1], block)
            gated[share, rows, :] = (query_v[rows, lanes].astype(F32) * conv).astype(BF)

        def send_gated(at, carry):
            piece = piece_of(at)
            gate_copy(0, piece, share, 0, 2, across).start()
            gate_copy(1, piece, share, 0, 1, sibling).start()
            return carry

        lax.fori_loop(0, 2 * STREAMS, send_gated, 0)

    def pass_on(piece, share):
        arrive(part(piece, 2, share), gate_rs.at[0, share, piece])
        gate_copy(2, piece, share, 2, 3, sibling).start()

    def gate_done(piece, share):
        arrive(part(piece, 1, share), gate_rs.at[1, share, piece])
        arrive(part(piece, 3, share), gate_rs.at[2, share, piece])

    local_done(9)
    inverse(0)
    inverse(1)
    gate(0)
    for step in (2, 6):
        send_weight_across(step, far, 1)

    def late_weights(depth, carry):
        send_weight_near(depth)
        return carry

    lax.fori_loop(0, 8, late_weights, 0)
    arrive(weights.at[0, pl.ds(0, 256), :], share_rs.at[0])
    share_weight(1)
    share_weight(7)

    def pass_first(at, carry):
        pass_on(piece_of(at), 0)
        return carry

    gate(1)
    lax.fori_loop(0, 2 * STREAMS, pass_first, 0)
    for step in (3, 5, 4, 0):
        send_weight_across(step, far, 2)
    arrive(weights.at[0, pl.ds(0, 256), :], share_rs.at[1])
    share_weight(2)
    share_weight(6)

    def wait_weight(step):
        depth = (z + step) % 8
        arrive(weights.at[depth, pl.ds(0, 896), :], weight_rs.at[depth])

    def term(piece, step):
        depth = (z + 7 - step) % 8 if piece // STREAMS == 0 else (z + 1 + step) % 8
        rows = rows_of(piece)
        values = jnp.concatenate([gated[at, rows, :] for at in range(4 * SHARES)], axis=1)
        return dot(values, weights[depth])

    def ring_copy(piece, step):
        depth = z_up if piece // STREAMS == 0 else z_down
        return pltpu.make_async_remote_copy(
            ring_send.at[piece, step],
            ring_recv.at[piece, step],
            ring_ss.at[piece],
            ring_rs.at[piece, step],
            device_id={"chan": chan_of(y_lo, depth, core), "seq": me},
            device_id_type=MESH,
        )

    wait_weight(1)
    wait_weight(7)
    for sub in range(STREAMS):
        for piece in (sub, sub + STREAMS):
            pass_on(piece, 1)
        for piece in (sub, sub + STREAMS):
            gate_done(piece, 0)
            gate_done(piece, 1)
            ring_send[piece, 0] = term(piece, 0).astype(BF)
            ring_copy(piece, 0).start()

    arrive(weights.at[0, pl.ds(0, 512), :], share_rs.at[2])
    for step in (3, 5, 4, 0):
        share_weight(step)

    def ring_step(step, carry):
        @pl.when(step < 4)
        def _():
            wait_weight(1 + step)

        @pl.when(step < 3)
        def _():
            wait_weight(7 - step)

        for sub in range(STREAMS):
            for piece in (sub, sub + STREAMS):
                own = term(piece, step)
                ring_copy(piece, step - 1).wait_recv()
                ring_send[piece, step] = (own + ring_recv[piece, step - 1].astype(F32)).astype(BF)
                ring_copy(piece, step).start()
        return carry

    lax.fori_loop(1, 7, ring_step, 0)
    wait_weight(0)
    for sub in range(STREAMS):
        for piece in (sub, sub + STREAMS):
            own = term(piece, 7)
            ring_copy(piece, 6).wait_recv()
            out[rows_of(piece), :] = (own + ring_recv[piece, 6].astype(F32)).astype(BF)

    for share in range(SHARES):
        arrive(prod_send.at[share, pl.ds(0, SEQ - 1)], prod_ss.at[share])
        arrive(conv_send.at[share, pl.ds(0, SEQ - 1)], conv_ss.at[share])
        for wave in range(WAVES):
            arrive(filt_send.at[share, wave, pl.ds(0, SEQ - 1)], filt_ss.at[share, wave])
        for kind in range(3):
            arrive(gated.at[0], gate_ss.at[kind, share])
    arrive(weights.at[pl.ds(0, 6)], weight_ss)
    for piece in range(2 * STREAMS):
        arrive(ring_send.at[piece], ring_ss.at[piece])


def body(query_input, key_input, value_input, filter_spectrum, out_weight):
    moves, lanes_table, rows_table, cols_table, twist, short_table = make_tables()
    anywhere = pl.BlockSpec(memory_space=pl.ANY)
    dma = pltpu.SemaphoreType.DMA
    mixed = pl.pallas_call(
        kernel,
        out_shape=pltpu.VMEM((1024, 256), BF),
        in_specs=[anywhere] * 11,
        out_specs=pl.BlockSpec(memory_space=pltpu.VMEM),
        scratch_shapes=[
            pltpu.VMEM((1024, 256), BF),
            pltpu.VMEM((1024, 256), BF),
            pltpu.VMEM((1024, 256), BF),
            pltpu.VMEM((128, SHORT, 2, 256), BF),
            pltpu.VMEM((3, 512, 512), BF),
            pltpu.VMEM((1024, 1024), BF),
            pltpu.VMEM((2, ORDER, ORDER // 2), BF),
            pltpu.VMEM((2, ORDER // 2, ORDER), BF),
            pltpu.VMEM((2, ORDER, LANES), F32),
            pltpu.VMEM((2, 2 * LANES, 2 * LANES), BF),
            pltpu.VMEM((SHORT, 64, 256), BF),
            pltpu.VMEM((WAVES, 2, SHORT, WAVE_ROWS, 256), BF),
            pltpu.VMEM((SHARES, SEQ, 64, LANES), BF),
            pltpu.VMEM((SHARES, SEQ, 64, LANES), BF),
            pltpu.VMEM((SHARES, WAVES, SEQ, 2, WAVE_ROWS, LANES), BF),
            pltpu.VMEM((SHARES, WAVES, SEQ, 2, WAVE_ROWS, LANES), BF),
            pltpu.VMEM((SHARES, ORDER, 2 * LANES), F32),
            pltpu.VMEM((512, LANES), F32),
            pltpu.VMEM((SHARES, SEQ, 64, LANES), BF),
            pltpu.VMEM((SHARES, SEQ, 64, LANES), BF),
            pltpu.VMEM((4 * SHARES, 1024, 128), BF),
            pltpu.VMEM((8, 1024, 256), BF),
            pltpu.VMEM((2 * STREAMS, 7, PIECE, 256), BF),
            pltpu.VMEM((2 * STREAMS, 7, PIECE, 256), BF),
            dma((10,)),
            dma((SHARES,)),
            dma((SHARES,)),
            dma((SHARES, WAVES)),
            dma((SHARES, WAVES)),
            dma((SHARES,)),
            dma((SHARES,)),
            dma,
            dma((8,)),
            dma((3,)),
            dma((3, SHARES)),
            dma((3, SHARES, 2 * STREAMS)),
            dma((2 * STREAMS,)),
            dma((2 * STREAMS, 7)),
        ],
        compiler_params=pltpu.CompilerParams(
            collective_id=0, has_side_effects=True, vmem_limit_bytes=58 * 2**20
        ),
        name="hyena",
    )(
        query_input,
        key_input,
        value_input,
        filter_spectrum,
        out_weight,
        jnp.asarray(moves),
        jnp.asarray(lanes_table),
        jnp.asarray(rows_table),
        jnp.asarray(cols_table),
        jnp.asarray(twist),
        jnp.asarray(short_table),
    )
    return mixed.T


def solution(mesh):
    in_specs = (
        P("seq", "chan"),
        P("seq", "chan"),
        P("seq", "chan"),
        P("seq", None, None, "chan"),
        P("chan", None),
    )
    return jax.shard_map(
        body, mesh=mesh, in_specs=in_specs, out_specs=P("chan", "seq"), check_vma=False
    )
```
